32 devices in a mesh: sweep: 2 (over x), env: 4 (over y, core), sec: 4 (over z).
Axes of the slice: x: 2, y: 2, z: 4, core: 2. Of those that a mesh axis runs over, the one named last changes fastest.
Arguments:
- corner: bfloat16 [1536, 768], P(('sweep', 'env')), parts along dimension 0, as said below
- edges: bfloat16 [72, 768, 768], P(('sweep', 'sec'), 'env'), parts along dimension 0, as said below
- projectors: bfloat16 [72, 768, 768], P(('sweep', 'sec'), 'env'), parts along dimension 0, as said below
- tile_counts: int32 [72], P(('sweep', 'sec')), parts along dimension 0, may hold values from 1 to 6, as said below
- cotangent: float32 [1536, 768], P(('sweep', 'env'), 'sec'), parts along dimension 0, may hold values from -6 to 6
Outputs:
- corner_new: float32 [1536, 768], P(('sweep', 'env'), 'sec'), parts along dimension 0
- corner_grad: float32 [1536, 768], P(('sweep', 'env'), 'sec'), parts along dimension 0
- edge_grad: float32 [72, 768, 768], P(('sweep', 'sec'), 'env'), parts along dimension 0
- proj_grad: float32 [72, 768, 768], P(('sweep', 'sec'), 'env'), parts along dimension 0
The draws below stay inside these ranges and needn't reach their ends.
There are 2 independent parts, one for each index of `sweep`. The reference program is written for one: setup_inputs(seed, part) draws one part's arguments, and reference() takes and returns one part's arrays. A program takes and returns all parts, laid end to end along the dimension named above; each array names one. Nothing has to cross between parts.
Inputs may be any that keep to these rules, and one draw needn't show every extreme that they name: `tile_counts`: each entry counts live tiles of 128 environment columns of one sector slice; in every draw some slice has all 6 tiles live. `corner`: Real-valued entries. `edges`: Real-valued entries. `projectors`: Real-valued entries.
All inputs are finite; a program needn't handle non-finite values.
Results may differ from the reference program's by a relative error of at most 0.018.
Values may be sent and summed in bfloat16 or wider, within the bound.
No kernel may reach another device: no remote copies, remote signals or barrier semaphores. Data moves between devices by JAX's collectives and lax.ppermute only.
A program may use at most 128 MiB of HBM per device.

```python
import jax
import jax.numpy as jnp
from jax import lax

CHI = 768
TILE = 128
K = 36
TILES = 6
N_ENV = 4


def weight_values(key, salt, shape, ramp):
    key = jax.random.fold_in(key, salt)
    first = jax.random.fold_in(key, 0)
    values = jnp.clip(jax.random.normal(first, shape, jnp.float32), -6.0, 6.0)
    position = jnp.arange(shape[-1], dtype=jnp.float32) / (shape[-1] - 1)
    column_factor = jnp.exp(ramp * position)
    return (values * column_factor * CHI ** (-0.5)).astype(jnp.bfloat16)


def corner_values(key):
    return weight_values(key, 21, (CHI, CHI), 0.0)


def edge_values(key):
    return weight_values(key, 22, (K, CHI, CHI), 0.0)


def projector_values(key, ramp):
    return weight_values(key, 23, (K, CHI, CHI), ramp)


def count_values(key):
    key = jax.random.fold_in(key, 11)
    first, second = jax.random.split(key)
    counts = jax.random.randint(first, (K,), 1, TILES + 1)
    where = jax.random.randint(second, (), 0, K)
    return counts.at[where].set(TILES).astype(jnp.int32)


def draw_corner(key, part):
    return corner_values(key)


def draw_edges(key, part):
    return edge_values(key)


def draw_projectors(key, part):
    ramp = 1.0986123
    return projector_values(key, ramp)


def draw_tile_counts(key, part):
    return count_values(key)


def draw_cotangent(key, part):
    own = jax.random.fold_in(key, 41)
    ramp = 1.0986123
    corner = corner_values(key).astype(jnp.float32)
    edges = edge_values(key)
    projectors = projector_values(key, ramp)
    counts = count_values(key)
    columns = jnp.arange(CHI, dtype=jnp.int32)

    def add_slice(total, item):
        edge, proj, count = item
        enlarged = jnp.dot(corner, edge.astype(jnp.float32), precision=lax.Precision.HIGHEST)
        enlarged = jnp.where(columns[None, :] < count * TILE, enlarged, 0.0)
        total = total + jnp.dot(proj.astype(jnp.float32).T, enlarged, precision=lax.Precision.HIGHEST)
        return (total, None)
    absorbed, unused = lax.scan(add_slice, jnp.zeros((CHI, CHI), jnp.float32), (edges, projectors, counts))
    direction = absorbed * (CHI / jnp.sqrt(jnp.sum(absorbed * absorbed)))
    keys = jax.random.split(own, 6)
    position = jnp.arange(CHI, dtype=jnp.float32) / (CHI - 1)
    anchor_points = jnp.linspace(0.0, 1.0, 6).astype(jnp.float32)
    gain = jnp.exp(jax.random.uniform(keys[0], (), jnp.float32, -0.9163, 0.9163))
    row_anchor = jax.random.uniform(keys[1], (6,), jnp.float32)
    col_anchor = jax.random.uniform(keys[3], (6,), jnp.float32)
    row_level = 0.5 * position + 0.35 * jnp.interp(position, anchor_points, row_anchor) + 0.15 * jax.random.uniform(keys[2], (CHI,), jnp.float32)
    col_level = 0.5 * position + 0.35 * jnp.interp(position, anchor_points, col_anchor) + 0.15 * jax.random.uniform(keys[4], (CHI,), jnp.float32)
    noise = jnp.clip(jax.random.normal(keys[5], (CHI, CHI), jnp.float32), -6.0, 6.0)
    row_scale = 0.15 * jnp.exp(2.3025851 * row_level)
    col_scale = 0.15 * jnp.exp(2.3025851 * col_level)
    values = gain * row_scale[:, None] * col_scale[None, :] * direction + noise
    return jnp.clip(values, -6.0, 6.0).astype(jnp.float32)


def setup_inputs(seed: int = 0, part: int = 0) -> dict:
    streams_of = jax.random.split(jax.random.key(seed), 6)
    part_keys = jax.random.split(jax.random.fold_in(streams_of[5], part), 6)
    corner = draw_corner(jax.random.fold_in(jax.random.fold_in(streams_of[5], part), 71), part)
    edges = draw_edges(jax.random.fold_in(jax.random.fold_in(streams_of[5], part), 71), part)
    projectors = draw_projectors(jax.random.fold_in(jax.random.fold_in(streams_of[5], part), 71), part)
    tile_counts = draw_tile_counts(jax.random.fold_in(jax.random.fold_in(streams_of[5], part), 71), part)
    cotangent = draw_cotangent(jax.random.fold_in(jax.random.fold_in(streams_of[5], part), 71), part)
    return {"corner": corner, "edges": edges, "projectors": projectors, "tile_counts": tile_counts, "cotangent": cotangent}


def reference(corner, edges, projectors, tile_counts, cotangent):
    columns = jnp.arange(CHI, dtype=jnp.int32)
    keep = columns[None, :] < (tile_counts * TILE)[:, None]

    def forward_step(total, item):
        edge, proj, alive = item
        enlarged = jnp.dot(corner, edge, preferred_element_type=jnp.float32)
        enlarged = jnp.where(alive[None, :], enlarged, 0.0).astype(jnp.bfloat16)
        total = total + jnp.dot(proj.T, enlarged, preferred_element_type=jnp.float32)
        return (total, enlarged)
    absorbed, enlarged_all = lax.scan(forward_step, jnp.zeros((CHI, CHI), jnp.float32), (edges, projectors, keep))
    scale = CHI / jnp.sqrt(jnp.sum(absorbed * absorbed))
    corner_new = scale * absorbed
    intersection = jnp.sum(cotangent * corner_new)
    absorbed_grad = (scale * (cotangent - corner_new * intersection / (CHI * CHI))).astype(jnp.bfloat16)
    rows_block = CHI // N_ENV
    corner_blocks = corner.reshape(N_ENV, rows_block, CHI).astype(jnp.float32)

    def backward_step(total, item):
        edge, proj, alive, enlarged = item
        enlarged_grad = jnp.dot(proj, absorbed_grad, preferred_element_type=jnp.float32)
        enlarged_grad = jnp.where(alive[None, :], enlarged_grad, 0.0).astype(jnp.bfloat16)
        proj_grad = jnp.dot(enlarged, absorbed_grad.T, preferred_element_type=jnp.float32)
        total = total + jnp.dot(enlarged_grad, edge.T, preferred_element_type=jnp.float32)
        grad_blocks = enlarged_grad.reshape(N_ENV, rows_block, CHI).astype(jnp.float32)
        pieces = jnp.einsum('rab,rac->rbc', corner_blocks, grad_blocks).astype(jnp.bfloat16)
        pieces = lax.optimization_barrier(pieces)
        edge_grad = lax.optimization_barrier(jnp.sum(pieces.astype(jnp.float32), axis=0))
        return (total, (edge_grad, proj_grad))
    corner_grad, outputs = lax.scan(backward_step, jnp.zeros((CHI, CHI), jnp.float32), (edges, projectors, keep, enlarged_all))
    edge_grad, proj_grad = outputs
    return (corner_new, corner_grad, edge_grad, proj_grad)
```

```python
import functools

import jax
import jax.numpy as jnp
from jax import lax
from jax.experimental import pallas as pl
from jax.experimental.pallas import tpu as pltpu
from jax.sharding import PartitionSpec as P

TILE = 128
F32, BF16 = jnp.float32, jnp.bfloat16
VMEM_LIMIT = 40 * 1024 * 1024


def swap(value, axis, offset):
    size = lax.axis_size(axis)
    return lax.ppermute(value, axis, [(i, i ^ offset) for i in range(size)])


def gather_blocks(own):
    blocks = [own]
    for m in range(1, lax.axis_size("env")):
        blocks.append(swap(blocks[m - 1], "env", 1) if m % 2 else swap(own, "env", m))
    return blocks


def after(value, *earlier):
    return lax.optimization_barrier((value, *earlier))[0]


def dot(a, b, dims=((1,), (0,))):
    return lax.dot_general(a, b, (dims, ((), ())), preferred_element_type=F32)


def call(kernel, name, grid, in_specs, out_specs, out_shape, scratch, flops, nbytes, prefetch, args):
    return pl.pallas_call(
        kernel,
        grid_spec=pltpu.PrefetchScalarGridSpec(
            num_scalar_prefetch=prefetch,
            grid=grid,
            in_specs=in_specs,
            out_specs=out_specs,
            scratch_shapes=scratch,
        ),
        out_shape=out_shape,
        name=name,
        compiler_params=pltpu.CompilerParams(vmem_limit_bytes=VMEM_LIMIT),
        cost_estimate=pl.CostEstimate(flops=flops, bytes_accessed=nbytes, transcendentals=0),
    )(*args)


def keep_columns(shape, first, count):
    return lax.broadcasted_iota(jnp.int32, shape, 1) + first < count * TILE


def whole(shape):
    return pl.BlockSpec(shape, lambda k, *s: (0,) * len(shape))


def per_slice(shape, index=0):
    return pl.BlockSpec((1, *shape), lambda k, *s: (k, 0, index))


def absorb_kernel(n, rows, first, me, counts, *refs):
    c_ref, e_refs, p_ref = refs[0], refs[1 : n + 1], refs[n + 1]
    enl_ref, keep_ref, send_ref, acc = refs[n + 2 :]
    k = pl.program_id(0)

    @pl.when(k == 0)
    def _():
        acc[...] = jnp.zeros_like(acc)

    x = dot(c_ref[0], e_refs[0][0])
    for m in range(1, n):
        x = x + dot(c_ref[m], e_refs[m][0])
    x = jnp.where(keep_columns(x.shape, first, counts[k]), x, 0.0).astype(BF16)
    enl_ref[0] = x
    acc[...] += dot(p_ref[0], x, ((0,), (0,)))

    @pl.when(k == pl.num_programs(0) - 1)
    def _():
        for j in range(n // 2):
            mine = pl.multiple_of((me[0] ^ (2 * j)) * rows, rows)
            other = pl.multiple_of((me[0] ^ (2 * j + 1)) * rows, rows)
            keep_ref[j] = acc[pl.ds(mine, rows), :]
            send_ref[j] = acc[pl.ds(other, rows), :].astype(BF16)


def absorb(me, counts, c_parts, e_blocks, edges, projectors, first, cols):
    n, rows = c_parts.shape[:2]
    slices, _, width = projectors.shape
    return call(
        functools.partial(absorb_kernel, n, rows, first),
        "absorb",
        (slices,),
        [whole(c_parts.shape), per_slice((rows, cols), first // cols)]
        + [per_slice((rows, cols))] * (n - 1)
        + [per_slice((rows, width))],
        [per_slice((rows, cols)), whole((n // 2, rows, cols)), whole((n // 2, rows, cols))],
        [
            jax.ShapeDtypeStruct((slices, rows, cols), BF16),
            jax.ShapeDtypeStruct((n // 2, rows, cols), F32),
            jax.ShapeDtypeStruct((n // 2, rows, cols), BF16),
        ],
        [pltpu.VMEM((width, cols), F32)],
        4 * slices * rows * width * cols,
        2 * slices * width * (cols + rows),
        2,
        (me, counts, c_parts, edges, *e_blocks[1:], projectors),
    )


def mix_kernel(n, refs_c, *refs):
    p_refs, out = refs[:n], refs[n]
    x = dot(refs_c[0], p_refs[0][0], ((0,), (0,)))
    for m in range(1, n):
        x = x + dot(refs_c[m], p_refs[m][0], ((0,), (0,)))
    out[0] = x.astype(BF16)


def mix(c_cols, p_blocks):
    n, rows = c_cols.shape[:2]
    slices, _, width = p_blocks[0].shape
    return call(
        functools.partial(mix_kernel, n),
        "mix",
        (slices,),
        [whole(c_cols.shape)] + [per_slice((rows, width))] * n,
        per_slice((rows, width)),
        jax.ShapeDtypeStruct((slices, rows, width), BF16),
        [],
        2 * slices * rows * width * width,
        2 * slices * width * (width + rows),
        0,
        (c_cols, *p_blocks),
    )


def fill(n, rows, me, g_refs, g):
    @pl.when(pl.program_id(0) == 0)
    def _():
        for m in range(n):
            at = pl.multiple_of((me[0] ^ m) * rows, rows)
            g[pl.ds(at, rows), :] = g_refs[m][...]


def corner_kernel(n, rows, me, counts, *refs):
    g_refs, p_ref, e_refs = refs[:n], refs[n], refs[n + 1 : 2 * n + 1]
    out, g, acc = refs[2 * n + 1 :]
    k = pl.program_id(0)
    fill(n, rows, me, g_refs, g)

    @pl.when(k == 0)
    def _():
        acc[...] = jnp.zeros_like(acc)

    x = dot(p_ref[0], g[...])
    x = jnp.where(keep_columns(x.shape, 0, counts[k]), x, 0.0).astype(BF16)
    for m in range(n):
        acc[m] += dot(x, e_refs[m][0], ((1,), (1,)))

    @pl.when(k == pl.num_programs(0) - 1)
    def _():
        for m in range(n):
            out[me[0] ^ m] = acc[m].astype(BF16)


def corner_part(me, counts, g_blocks, projectors, e_blocks):
    n = len(g_blocks)
    slices, rows, width = projectors.shape
    return call(
        functools.partial(corner_kernel, n, rows),
        "corner_part",
        (slices,),
        [whole((rows, width))] * n + [per_slice((rows, width))] * (n + 1),
        whole((n, rows, rows)),
        jax.ShapeDtypeStruct((n, rows, rows), BF16),
        [pltpu.VMEM((width, width), BF16), pltpu.VMEM((n, rows, rows), F32)],
        4 * slices * rows * width * width,
        2 * slices * width * (width + rows),
        2,
        (me, counts, *g_blocks, projectors, *e_blocks),
    )


def grads_kernel(n, rows, parts, me, counts, *refs):
    g_refs, q_ref, enl_refs = refs[:n], refs[n], refs[n + 1 : n + 1 + len(parts)]
    edge, proj, g = refs[n + 1 + len(parts) :]
    fill(n, rows, me, g_refs, g)
    k = pl.program_id(0)
    x = dot(q_ref[0], g[...])
    edge[0] = jnp.where(keep_columns(x.shape, 0, counts[k]), x, 0.0)
    y = None
    for (first, cols), enl in zip(parts, enl_refs):
        z = dot(enl[0], g[:, first : first + cols], ((1,), (1,)))
        y = z if y is None else y + z
    proj[0] = y


def grads(me, counts, g_blocks, q, enlarged, parts):
    n = len(g_blocks)
    slices, rows, width = q.shape
    return call(
        functools.partial(grads_kernel, n, rows, parts),
        "grads",
        (slices,),
        [whole((rows, width))] * n
        + [per_slice((rows, width))]
        + [per_slice((rows, cols)) for _, cols in parts],
        [per_slice((rows, width))] * 2,
        [jax.ShapeDtypeStruct((slices, rows, width), F32)] * 2,
        [pltpu.VMEM((width, width), BF16)],
        4 * slices * rows * width * width,
        12 * slices * width * rows,
        2,
        (me, counts, *g_blocks, q, *enlarged),
    )


def per_device(corner, edges, projectors, tile_counts, cotangent):
    n, n_sec = lax.axis_size("env"), lax.axis_size("sec")
    e, s = lax.axis_index("env"), lax.axis_index("sec")
    slices, rows, width = edges.shape
    cols = cotangent.shape[1]
    me = jnp.reshape(e, (1,)).astype(jnp.int32)
    parts = ((0, width // 3 * 2), (width // 3 * 2, width // 3))

    e_parts, earlier = [], None
    for first, size in parts:
        piece = edges[:, :, first : first + size]
        if earlier is not None:
            piece = after(piece, earlier)
        e_parts.append(gather_blocks(piece))
        earlier = e_parts[-1][2]

    c_parts = [lax.dynamic_slice_in_dim(corner, (e ^ m) * rows, rows, 1) for m in range(n)]
    c_cols = jnp.stack([c_parts[0]] + [swap(c_parts[m], "env", m) for m in range(1, n)])
    c_parts = jnp.stack(c_parts)

    cot_blocks = [cotangent] + [swap(cotangent, "sec", m) for m in range(1, n_sec)]
    cot_rows = jnp.concatenate(
        [
            functools.reduce(
                lambda a, m: jnp.where((s ^ m) == q, cot_blocks[m], a), range(1, n_sec), cot_blocks[0]
            )
            for q in range(n_sec)
        ],
        axis=1,
    )

    enlarged, absorbed = [], []
    for (first, size), blocks in zip(parts, e_parts):
        enl, keep, send = absorb(me, tile_counts, c_parts, blocks, edges, projectors, first, size)
        enlarged.append(enl)
        total = keep + swap(send, "env", 1).astype(F32)
        moved = total.astype(BF16)
        total = total[0]
        for j in range(1, n // 2):
            total = total + swap(moved[j], "env", 2 * j).astype(F32)
        moved = total.astype(BF16)
        total = moved.astype(F32)
        for m in range(1, n_sec):
            total = total + swap(moved, "sec", m).astype(F32)
        absorbed.append(total)
    absorbed = jnp.concatenate(absorbed, axis=1)

    third = slices // 3
    mixed, earlier = [], e_parts[-1][2]
    for at in range(0, slices, third):
        piece = after(projectors[at : at + third], earlier)
        blocks = gather_blocks(piece)
        earlier = blocks[2]
        mixed.append(mix(c_cols, blocks))
    mixed = jnp.concatenate(mixed, axis=0)

    sums = jnp.stack([jnp.sum(absorbed * absorbed), jnp.sum(cot_rows * absorbed)])
    own = sums
    for m in range(2, n, 2):
        sums = sums + swap(own, "env", m)
    sums = sums + swap(sums, "env", 1)
    scale = width / jnp.sqrt(sums[0])
    intersection = scale * sums[1]
    corner_new = scale * absorbed
    grad_rows = (scale * (cot_rows - corner_new * intersection / (width * width))).astype(BF16)
    corner_new = lax.dynamic_slice_in_dim(corner_new, s * cols, cols, 1)
    g_blocks = gather_blocks(grad_rows)

    e_full = [edges] + [
        jnp.concatenate([blocks[m] for blocks in e_parts], axis=2) for m in range(1, n)
    ]
    part = corner_part(me, tile_counts, g_blocks, projectors, e_full)
    part = jnp.transpose(part, (1, 0, 2)).reshape(rows, width)
    corner_grad = lax.dynamic_slice_in_dim(part, s * cols, cols, 1).astype(F32)
    for m in range(1, n_sec):
        piece = lax.dynamic_slice_in_dim(part, (s ^ m) * cols, cols, 1)
        corner_grad = corner_grad + swap(piece, "sec", m).astype(F32)

    edge_grad, proj_grad = grads(me, tile_counts, g_blocks, mixed, enlarged, parts)
    return (corner_new, corner_grad, edge_grad, proj_grad)


def solution(mesh):
    placed = (
        P(("sweep", "env"), None),
        P(("sweep", "sec"), "env", None),
        P(("sweep", "sec"), "env", None),
        P(("sweep", "sec")),
        P(("sweep", "env"), "sec"),
    )
    return jax.shard_map(
        per_device,
        mesh=mesh,
        in_specs=placed,
        out_specs=(
            P(("sweep", "env"), "sec"),
            P(("sweep", "env"), "sec"),
            P(("sweep", "sec"), "env", None),
            P(("sweep", "sec"), "env", None),
        ),
        check_vma=False,
    )
```

```python
import functools

import jax
import jax.numpy as jnp
from jax import lax
from jax.experimental import pallas as pl
from jax.experimental.pallas import tpu as pltpu
from jax.sharding import PartitionSpec as P

TILE = 128
F32, BF16 = jnp.float32, jnp.bfloat16
VMEM_LIMIT = 40 * 1024 * 1024


def swap(value, axis, offset):
    size = lax.axis_size(axis)
    return lax.ppermute(value, axis, [(i, i ^ offset) for i in range(size)])


def after(value, *earlier):
    return lax.optimization_barrier((value, *earlier))[0]


def dot(a, b, dims=((1,), (0,))):
    return lax.dot_general(a, b, (dims, ((), ())), preferred_element_type=F32)


def call(kernel, name, grid, in_specs, out_specs, out_shape, scratch, flops, nbytes, prefetch, args):
    return pl.pallas_call(
        kernel,
        grid_spec=pltpu.PrefetchScalarGridSpec(
            num_scalar_prefetch=prefetch,
            grid=grid,
            in_specs=in_specs,
            out_specs=out_specs,
            scratch_shapes=scratch,
        ),
        out_shape=out_shape,
        name=name,
        compiler_params=pltpu.CompilerParams(vmem_limit_bytes=VMEM_LIMIT),
        cost_estimate=pl.CostEstimate(flops=1000, bytes_accessed=1000, transcendentals=0),
    )(*args)


def keep_columns(shape, first, count):
    return lax.broadcasted_iota(jnp.int32, shape, 1) + first < count * TILE


def whole(shape):
    return pl.BlockSpec(shape, lambda k, *s: (0,) * len(shape))


def group(size, shape, column=0, first=0):
    return pl.BlockSpec((size, *shape), lambda k, *s: (k + first, 0, column))


def sizes(mesh_rows, width):
    n, n_sec = lax.axis_size("env"), lax.axis_size("sec")
    return n, n_sec, n // 2, width // (n * n_sec)


def place(me, m_core, m_sec, m_y, n_sec, n_y, piece):
    core, y = me[0] & 1, me[0] >> 1
    at = (((core ^ m_core) * n_sec + (me[1] ^ m_sec)) * n_y + (y ^ m_y)) * piece
    return pl.multiple_of(at, piece)


def fetch(per, ref, buffer, rows, sems):
    copies = []
    for k in range(ref.shape[0] // per):
        at = pl.ds(k * per, per)
        copies.append(pltpu.make_async_copy(ref.at[at], buffer.at[at, rows], sems.at[k]))
        copies[-1].start()
    return copies


def absorb_kernel(n, n_sec, piece, per, me, counts, c_ref, *refs):
    e_refs, p_ref = refs[:n], refs[n]
    enl_ref, keep_ref, send_ref, held, p_held, enl, acc, sems, out_sems = refs[n + 1 :]
    n_y = n // 2
    slices, rows, width = p_ref.shape
    copies = [
        fetch(per, e_refs[m], held, pl.ds(m * rows, rows), sems.at[m]) for m in range(n)
    ]
    p_copies = fetch(per, p_ref, p_held, pl.ds(0, rows), sems.at[n])
    stores = []
    for k in range(slices // per):
        for m in range(n):
            copies[m][k].wait()
        for i in range(k * per, k * per + per):
            x = dot(c_ref[...], held[i])
            enl[i] = jnp.where(keep_columns(x.shape, 0, counts[i]), x, 0.0).astype(BF16)
        at = pl.ds(k * per, per)
        stores.append(pltpu.make_async_copy(enl.at[at], enl_ref.at[at], out_sems.at[k]))
        stores[-1].start()
    for copy in p_copies:
        copy.wait()
    half = width // 2
    for first in (0, half):
        acc[first : first + half, :] = dot(
            p_held[:, :, first : first + half].reshape(slices * rows, half),
            enl[...].reshape(slices * rows, width),
            ((0,), (0,)),
        )
    if piece % 16:
        keep_ref[...] = acc[...]
        send_ref[...] = acc[...].astype(BF16)
    else:
        for m_sec in range(n_sec):
            for m_y in range(n_y):
                at = (m_sec * n_y + m_y) * piece
                for m_core, ref in ((0, keep_ref), (1, send_ref)):
                    part = acc[pl.ds(place(me, m_core, m_sec, m_y, n_sec, n_y, piece), piece), :]
                    ref[at : at + piece] = part.astype(ref.dtype)
    for store in stores:
        store.wait()


SCALARS = pl.BlockSpec(memory_space=pltpu.SMEM)
ARRAY = pl.BlockSpec(memory_space=pltpu.VMEM)
FAR = pl.BlockSpec(memory_space=pl.ANY)


def at_once(kernel, name, out_shape, out_specs, scratch, scalars, near, far):
    return pl.pallas_call(
        kernel,
        in_specs=[SCALARS] * len(scalars) + [ARRAY] * len(near) + [FAR] * len(far),
        out_specs=out_specs,
        out_shape=out_shape,
        scratch_shapes=scratch,
        name=name,
        compiler_params=pltpu.CompilerParams(vmem_limit_bytes=VMEM_LIMIT),
        cost_estimate=pl.CostEstimate(flops=1000, bytes_accessed=1000, transcendentals=0),
    )(*scalars, *near, *far)


def absorb(me, counts, c_parts, e_blocks, projectors):
    slices, rows, width = projectors.shape
    n, n_sec, n_y, piece = sizes(rows, width)
    per = 3 if slices % 3 == 0 else 1
    half = (width if piece % 16 else width // 2, width)
    held = (slices, rows, width)
    enlarged, keep, send = at_once(
        functools.partial(absorb_kernel, n, n_sec, piece, per),
        "absorb",
        [
            jax.ShapeDtypeStruct(held, BF16),
            jax.ShapeDtypeStruct(half, F32),
            jax.ShapeDtypeStruct(half, BF16),
        ],
        [FAR, ARRAY, ARRAY],
        [
            pltpu.VMEM((slices, width, width), BF16),
            pltpu.VMEM(held, BF16),
            pltpu.VMEM(held, BF16),
            pltpu.VMEM((width, width), F32),
            pltpu.SemaphoreType.DMA((n + 1, slices // per)),
            pltpu.SemaphoreType.DMA((slices // per,)),
        ],
        (me, counts),
        (c_parts,),
        (*e_blocks, projectors),
    )
    if piece % 16:
        keep = relative(keep, me, n_sec, n_y)[0]
        send = relative(send, me, n_sec, n_y)[1]
    shape = (n_sec, n_y * piece, width)
    return enlarged, keep.reshape(shape), send.reshape(shape)


def relative(value, me, n_sec, n_y):
    rows, cols = value.shape
    value = value.reshape(2, n_sec, n_y, rows // (2 * n_sec * n_y), cols)
    value = jnp.take(value, jnp.arange(2) ^ (me[0] & 1), axis=0)
    value = jnp.take(value, jnp.arange(n_sec) ^ me[1], axis=1)
    return jnp.take(value, jnp.arange(n_y) ^ (me[0] >> 1), axis=2).reshape(2, rows // 2, cols)


class Order:
    def __init__(self):
        self.last = None

    def __call__(self, step, *args):
        if self.last is not None:
            args = lax.optimization_barrier((*args, self.last))[:-1]
        out = step(*args)
        self.last = jax.tree.leaves(out)[0]
        return out


def add_core(keep, arrived):
    total = keep + arrived.astype(F32)
    return total.astype(BF16), total[0]


def add_sec(total, *arrived):
    for block in arrived:
        total = total + block.astype(F32)
    total = total.reshape(lax.axis_size("env") // 2, -1, total.shape[-1])
    return total.astype(BF16), total[0]


def add_chips(total, *arrived):
    for block in arrived:
        total = total + block.astype(F32)
    return total.astype(BF16)


def join(*blocks):
    return jnp.concatenate(blocks, axis=0)


def to_sec(blocks):
    return [swap(blocks[m], "sec", m) for m in range(1, lax.axis_size("sec"))]


def to_chips(blocks):
    return [swap(blocks[m], "env", 2 * m) for m in range(1, lax.axis_size("env") // 2)]


def all_chips(block):
    return [block] + to_chips([block] * (lax.axis_size("env") // 2))


def all_sec(block):
    return [block] + to_sec([block] * lax.axis_size("sec"))


def gradient_kernel(n, n_sec, piece, rows, me, *refs):
    cot_refs, blocks = refs[:n], refs[n : n + 2 * n_sec]
    g_ref, own_ref, full, cot_ref = refs[n + 2 * n_sec :]
    width = full.shape[0]
    n_y = n // 2
    for m in range(n):
        to = pl.multiple_of((me[0] ^ m) * rows, rows)
        cot_ref[pl.ds(to, rows), :] = cot_refs[m][0]
    for m_core in range(2):
        for m_sec in range(n_sec):
            block = blocks[m_core * n_sec + m_sec]
            if piece % 16:
                at = (m_core * n_sec + m_sec) * n_y * piece
                full[at : at + n_y * piece] = block[...]
                continue
            for m_y in range(n_y):
                to = place(me, m_core, m_sec, m_y, n_sec, n_y, piece)
                full[pl.ds(to, piece), :] = block[m_y * piece : (m_y + 1) * piece]
    step = 16
    zero = jnp.zeros((step, width), F32)

    def add(i, sums):
        at = pl.ds(pl.multiple_of(i * step, step), step)
        x, c = full[at, :].astype(F32), cot_ref[at, :].astype(F32)
        return sums[0] + x * x, sums[1] + c * x

    norm_sq, cross = lax.fori_loop(0, width // step, add, (zero, zero), unroll=2)
    norm_sq = jnp.sum(norm_sq, keepdims=True)
    cross = jnp.sum(cross, keepdims=True)
    scale = width / jnp.sqrt(norm_sq)
    ratio = scale * cross * scale / (width * width)

    def write(i, _):
        at = pl.ds(pl.multiple_of(i * step, step), step)
        x, c = full[at, :].astype(F32), cot_ref[at, :].astype(F32)
        g_ref[at, :] = (scale * (c - x * ratio)).astype(BF16)
        return _

    lax.fori_loop(0, width // step, write, 0, unroll=2)
    own = full[pl.ds(pl.multiple_of(me[0] * rows, rows), rows), :]
    own_ref[...] = own.astype(F32) * scale


def gradient(me, rows, cots, at, halves):
    width = cots[0].shape[2]
    n, n_sec, n_y, piece = sizes(rows, width)
    return call(
        functools.partial(gradient_kernel, n, n_sec, piece, rows),
        "gradient",
        (1,),
        [pl.BlockSpec((1, rows, width), lambda k, *s: (at, 0, 0))] * n
        + [whole(h.shape) for h in halves],
        [whole((width, width)), whole((rows, width))],
        [jax.ShapeDtypeStruct((width, width), BF16), jax.ShapeDtypeStruct((rows, width), F32)],
        [pltpu.VMEM((width, width), BF16)] * 2,
        8 * width * width,
        10 * width * width,
        1,
        (me, *cots, *halves),
    )


def corner_kernel(n, n_sec, per, me, counts, g_ref, p_ref, *refs):
    e_refs, (out, held, p_held, grad, acc, sems) = refs[:n], refs[n:]
    slices, rows, width = p_ref.shape
    cols = width // n_sec
    p_copies = fetch(per, p_ref, p_held, pl.ds(0, rows), sems.at[n])
    copies = [
        fetch(per, e_refs[m], held, pl.ds(m * rows, rows), sems.at[m]) for m in range(n)
    ]
    for k in range(slices // per):
        p_copies[k].wait()
        x = dot(p_held[k * per : k * per + per].reshape(per * rows, width), g_ref[...])
        for i in range(per):
            part = x[i * rows : (i + 1) * rows]
            keep = keep_columns(part.shape, 0, counts[k * per + i])
            grad[k * per + i] = jnp.where(keep, part, 0.0).astype(BF16)
    for m in range(n):
        for copy in copies[m]:
            copy.wait()
        x = None
        for k in range(slices):
            y = dot(held[k, m * rows : (m + 1) * rows], grad[k], ((1,), (1,)))
            x = y if x is None else x + y
        acc[pl.ds(pl.multiple_of((me[0] ^ m) * rows, rows), rows), :] = x
    for m in range(n_sec):
        at = pl.multiple_of((me[1] ^ m) * cols, cols)
        out[m] = acc[pl.ds(at, cols), :].astype(BF16)


def corner_part(me, counts, g, projectors, e_blocks):
    slices, rows, width = projectors.shape
    n, n_sec = lax.axis_size("env"), lax.axis_size("sec")
    held = (slices, rows, width)
    per = 3 if slices % 3 == 0 else 1
    return at_once(
        functools.partial(corner_kernel, n, n_sec, per),
        "corner_part",
        jax.ShapeDtypeStruct((n_sec, width // n_sec, rows), BF16),
        ARRAY,
        [
            pltpu.VMEM((slices, width, width), BF16),
            pltpu.VMEM(held, BF16),
            pltpu.VMEM(held, BF16),
            pltpu.VMEM((width, rows), F32),
            pltpu.SemaphoreType.DMA((n + 1, slices // per)),
        ],
        (me, counts),
        (g,),
        (projectors, *e_blocks),
    )


def early_kernel(per, counts, g_ref, enl_ref, q_ref, proj, edge):
    k = pl.program_id(0)
    for i in range(per):
        proj[i] = dot(enl_ref[i], g_ref[...], ((1,), (1,)))
    x = dot(q_ref[0], g_ref[...])
    edge[0] = jnp.where(keep_columns(x.shape, 0, counts[k]), x, 0.0)


def early_gradients(counts, g, enlarged, q):
    slices, rows, width = enlarged.shape
    steps = q.shape[0]
    per = slices // steps
    out = jax.ShapeDtypeStruct((slices, rows, width), F32)
    return call(
        functools.partial(early_kernel, per),
        "early_gradients",
        (steps,),
        [whole((width, width)), group(per, (rows, width)), group(1, (rows, width))],
        [group(per, (rows, width)), group(1, (rows, width))],
        [out, out],
        [],
        2 * slices * rows * width * width,
        6 * slices * width * rows,
        1,
        (counts, g, enlarged, q),
    )


def turn(n, c_refs, turned):
    @pl.when(pl.program_id(0) == 0)
    def _():
        for m in range(n):
            turned[m] = c_refs[m].T


def mixed(n, turned, p_refs, i):
    q = dot(turned[0], p_refs[0][i])
    for m in range(1, n):
        q = q + dot(turned[m], p_refs[m][i])
    return q.astype(BF16)


def mix_kernel(n, per, c_ref, *refs):
    p_refs, out, turned = refs[:n], refs[n], refs[n + 1]
    turn(n, c_ref, turned)
    for i in range(per):
        out[i] = mixed(n, turned, p_refs, i)


def mix(c_cols, p_blocks, slices):
    n, rows = c_cols.shape[:2]
    width = p_blocks[0].shape[2]
    return call(
        functools.partial(mix_kernel, n, slices),
        "mix",
        (1,),
        [whole(c_cols.shape)] + [group(slices, (rows, width))] * n,
        group(slices, (rows, width)),
        jax.ShapeDtypeStruct((slices, rows, width), BF16),
        [pltpu.VMEM(c_cols.shape, BF16)],
        2 * slices * rows * width * width,
        2 * slices * width * (width + rows),
        0,
        (c_cols, *p_blocks),
    )


def late_edge_kernel(n, first, per, counts, g_ref, c_ref, *refs):
    p_refs, out, turned = refs[:n], refs[-2], refs[-1]
    k = pl.program_id(0)
    turn(n, c_ref, turned)
    for i in range(per):
        x = dot(mixed(n, turned, p_refs, i), g_ref[...])
        keep = keep_columns(x.shape, 0, counts[first + k * per + i])
        out[i] = jnp.where(keep, x, 0.0)


def late_edge_gradient(result, shape, counts, g, c_cols, p_blocks, first):
    n, rows = c_cols.shape[:2]
    slices, _, width = p_blocks[0].shape
    per = 3 if slices % 3 == 0 else 1
    return into(
        functools.partial(late_edge_kernel, n, first, per),
        "late_edge_gradient",
        result,
        shape,
        first,
        slices,
        [whole((width, width)), whole(c_cols.shape)] + [group(per, (rows, width))] * n,
        [pltpu.VMEM(c_cols.shape, BF16)],
        (counts, g, c_cols, *p_blocks),
        per,
    )


def into(kernel, name, result, shape, first, slices, in_specs, scratch, args, per):
    aliases = {}
    if result is not None:
        aliases = {len(args): 0}
        in_specs = in_specs + [pl.BlockSpec(memory_space=pl.ANY)]
        args = (*args, result)
    return pl.pallas_call(
        kernel,
        grid_spec=pltpu.PrefetchScalarGridSpec(
            num_scalar_prefetch=1,
            grid=(slices // per,),
            in_specs=in_specs,
            out_specs=group(per, shape[1:], 0, first // per),
            scratch_shapes=scratch,
        ),
        out_shape=jax.ShapeDtypeStruct(shape, F32),
        input_output_aliases=aliases,
        name=name,
        compiler_params=pltpu.CompilerParams(vmem_limit_bytes=VMEM_LIMIT),
        cost_estimate=pl.CostEstimate(flops=1000, bytes_accessed=1000, transcendentals=0),
    )(*args)


def cotangent_order(*blocks):
    n_sec, s = lax.axis_size("sec"), lax.axis_index("sec")
    ordered = []
    for q in range(n_sec):
        block = blocks[0]
        for m in range(1, n_sec):
            block = jnp.where((s ^ m) == q, blocks[m], block)
        ordered.append(block)
    return jnp.concatenate(ordered, axis=1)


def per_device(corner, edges, projectors, tile_counts, cotangent):
    n, n_sec = lax.axis_size("env"), lax.axis_size("sec")
    e, s = lax.axis_index("env"), lax.axis_index("sec")
    slices, rows, width = edges.shape
    cols = cotangent.shape[1]
    piece = width // (n * n_sec)
    me = jnp.stack([e, s]).astype(jnp.int32)
    core, y = e & 1, e >> 1

    def from_chips(value):
        return to_chips([value] * (n // 2))

    def both_cores(arrived):
        return [b for block in arrived for b in (block, swap(block, "env", 1))]

    def barrier(value, *earlier):
        return lax.optimization_barrier((value, earlier))[0]

    far = from_chips(edges)
    cot = cotangent.astype(BF16)
    cot = cotangent_order(cot, *to_sec([cot] * n_sec))
    third = slices // 3
    pieces = [
        jnp.concatenate([projectors[:third], corner[None], cot[None]], axis=0),
        projectors[third:],
    ]
    p_blocks = [[p, swap(p, "env", 1)] for p in pieces]
    c_parts = jnp.concatenate(
        [lax.dynamic_slice_in_dim(corner, (e ^ m) * rows, rows, 1) for m in range(n)], axis=1
    )
    e_near = swap(edges, "env", 1)
    far = barrier(far, p_blocks, c_parts, e_near)
    p_far = [from_chips(barrier(pieces[0], far))]
    e_blocks = [edges, e_near, *both_cores(far)]

    order = Order()

    enlarged, keep, send = order(
        lambda *f: absorb(me, tile_counts, c_parts, f, projectors), *e_blocks)
    moved, total = order(add_core, keep, swap(send, "env", 1))
    sec = to_sec(moved)
    total = barrier(total, p_far[0])
    moved, total = order(add_sec, total, *sec)
    own = order(add_chips, total, *to_chips(moved))
    some = order(join, *all_chips(own))
    half = all_sec(some)
    p_far += [from_chips(barrier(p, some)) for p in pieces[1:]]
    p_blocks[0] += both_cores(barrier(p_far[0], some))
    cots = p_blocks[0]
    c_cols = jnp.stack(
        [lax.dynamic_slice_in_dim(p[third], e * rows, rows, 1) for p in p_blocks[0]]
    )
    q = order(lambda c: mix(c, p_blocks[0], third), c_cols)
    half = barrier(half, order.last)
    halves = half + [swap(h, "env", 1) for h in half]
    if piece % 16:
        halves = list(
            relative(jnp.concatenate(halves), me, n_sec, n // 2).reshape(2 * n_sec, -1, width))
    g, corner_new = order(lambda *h: gradient(me, rows, cots, third + 1, h), *halves)
    corner_new = lax.dynamic_slice_in_dim(corner_new, s * cols, cols, 1)

    part = order(lambda g: corner_part(me, tile_counts, g, projectors, e_blocks), g)
    moved = to_sec(part)
    proj_grad, edge_grad = order(
        lambda g: early_gradients(tile_counts, g, enlarged, q), g)
    corner_grad = order(
        lambda *b: sum((x.astype(F32) for x in b[1:]), b[0].astype(F32)).T, part[0], *moved)
    p_blocks[1] += both_cores(barrier(p_far[1], corner_grad))
    edge_grad = order(
        lambda r, *p: late_edge_gradient(
            r, (slices, rows, width), tile_counts, g, c_cols, p, third), edge_grad, *p_blocks[1])
    return (corner_new, corner_grad, edge_grad, proj_grad)


def solution(mesh):
    placed = (
        P(("sweep", "env"), None),
        P(("sweep", "sec"), "env", None),
        P(("sweep", "sec"), "env", None),
        P(("sweep", "sec")),
        P(("sweep", "env"), "sec"),
    )
    return jax.shard_map(
        per_device,
        mesh=mesh,
        in_specs=placed,
        out_specs=(
            P(("sweep", "env"), "sec"),
            P(("sweep", "env"), "sec"),
            P(("sweep", "sec"), "env", None),
            P(("sweep", "sec"), "env", None),
        ),
        check_vma=False,
    )
```

```python
import functools

import jax
import jax.numpy as jnp
from jax import lax
from jax.experimental import pallas as pl
from jax.experimental.pallas import tpu as pltpu
from jax.sharding import PartitionSpec as P

TILE = 128
F32, BF16 = jnp.float32, jnp.bfloat16
VMEM_LIMIT = 40 * 1024 * 1024


def swap(value, axis, offset):
    size = lax.axis_size(axis)
    return lax.ppermute(value, axis, [(i, i ^ offset) for i in range(size)])


def after(value, *earlier):
    return lax.optimization_barrier((value, *earlier))[0]


def dot(a, b, dims=((1,), (0,))):
    return lax.dot_general(a, b, (dims, ((), ())), preferred_element_type=F32)


def call(kernel, name, grid, in_specs, out_specs, out_shape, scratch, flops, nbytes, prefetch, args):
    return pl.pallas_call(
        kernel,
        grid_spec=pltpu.PrefetchScalarGridSpec(
            num_scalar_prefetch=prefetch,
            grid=grid,
            in_specs=in_specs,
            out_specs=out_specs,
            scratch_shapes=scratch,
        ),
        out_shape=out_shape,
        name=name,
        compiler_params=pltpu.CompilerParams(vmem_limit_bytes=VMEM_LIMIT),
        cost_estimate=pl.CostEstimate(flops=1000, bytes_accessed=1000, transcendentals=0),
    )(*args)


def keep_columns(shape, first, count):
    return lax.broadcasted_iota(jnp.int32, shape, 1) + first < count * TILE


def whole(shape):
    return pl.BlockSpec(shape, lambda k, *s: (0,) * len(shape))


def group(size, shape, column=0, first=0):
    return pl.BlockSpec((size, *shape), lambda k, *s: (k + first, 0, column))


def sizes(mesh_rows, width):
    n, n_sec = lax.axis_size("env"), lax.axis_size("sec")
    return n, n_sec, n // 2, width // (n * n_sec)


def place(me, m_core, m_sec, m_y, n_sec, n_y, piece):
    core, y = me[0] & 1, me[0] >> 1
    at = (((core ^ m_core) * n_sec + (me[1] ^ m_sec)) * n_y + (y ^ m_y)) * piece
    return pl.multiple_of(at, piece)


def fetch(per, ref, buffer, rows, sems):
    copies = []
    for k in range(ref.shape[0] // per):
        at = pl.ds(k * per, per)
        copies.append(pltpu.make_async_copy(ref.at[at], buffer.at[at, rows], sems.at[k]))
        copies[-1].start()
    return copies


def begin_kernel(per, c_ref, own, near, out):
    for i in range(per):
        out[i] = dot(c_ref[0], own[i]) + dot(c_ref[1], near[i])


def begin(c_parts, own, near):
    slices, rows, width = own.shape
    per = 3 if slices % 3 == 0 else 1
    return call(
        functools.partial(begin_kernel, per),
        "begin",
        (slices // per,),
        [whole(c_parts.shape)] + [group(per, (rows, width))] * 2,
        group(per, (c_parts.shape[1], width)),
        jax.ShapeDtypeStruct((slices, c_parts.shape[1], width), F32),
        [],
        0,
        0,
        0,
        (c_parts, own, near),
    )


def absorb_kernel(n, n_sec, piece, per, me, counts, c_ref, p_ref, begun, fwd, *refs):
    far_refs, (enl_ref, keep_ref, send_ref, held, enl, acc, sems, out_sems) = refs[:-8], refs[-8:]
    n_y = n // 2
    slices, rows, width = p_ref.shape
    copies = [
        fetch(per, far_refs[m], held.at[m], pl.ds(0, rows), sems.at[m]) for m in range(n - 3)
    ]
    stores = []
    for k in range(slices // per):
        at = pl.ds(k * per, per)
        for m in range(n - 3):
            copies[m][k].wait()
        for i in range(k * per, k * per + per):
            x = begun[i] + dot(c_ref[n - 1], fwd[i])
            for m in range(n - 3):
                x = x + dot(c_ref[2 + m], held[m, i])
            enl[i] = jnp.where(keep_columns(x.shape, 0, counts[i]), x, 0.0).astype(BF16)
        stores.append(pltpu.make_async_copy(enl.at[at], enl_ref.at[at], out_sems.at[k]))
        stores[-1].start()
    half = width // 2
    for first in (0, half):
        acc[first : first + half, :] = dot(
            p_ref[:, :, first : first + half].reshape(slices * rows, half),
            enl[...].reshape(slices * rows, width),
            ((0,), (0,)),
        )
    if piece % 16:
        keep_ref[...] = acc[...]
        send_ref[...] = acc[...].astype(BF16)
    else:
        for m_sec in range(n_sec):
            for m_y in range(n_y):
                at = (m_sec * n_y + m_y) * piece
                for m_core, ref in ((0, keep_ref), (1, send_ref)):
                    part = acc[pl.ds(place(me, m_core, m_sec, m_y, n_sec, n_y, piece), piece), :]
                    ref[at : at + piece] = part.astype(ref.dtype)
    for store in stores:
        store.wait()


SCALARS = pl.BlockSpec(memory_space=pltpu.SMEM)
ARRAY = pl.BlockSpec(memory_space=pltpu.VMEM)
FAR = pl.BlockSpec(memory_space=pl.ANY)


def at_once(
    kernel, name, out_shape, out_specs, scratch, scalars, near, far, aliases=None, vmem=VMEM_LIMIT, nbytes=1000
):
    return pl.pallas_call(
        kernel,
        in_specs=[SCALARS] * len(scalars) + [ARRAY] * len(near) + [FAR] * len(far),
        out_specs=out_specs,
        out_shape=out_shape,
        scratch_shapes=scratch,
        input_output_aliases=aliases or {},
        name=name,
        compiler_params=pltpu.CompilerParams(vmem_limit_bytes=vmem),
        cost_estimate=pl.CostEstimate(flops=1000, bytes_accessed=nbytes, transcendentals=0),
    )(*scalars, *near, *far)


def absorb(me, counts, c_parts, begun, e_far, projectors):
    slices, rows, width = projectors.shape
    n, n_sec, n_y, piece = sizes(rows, width)
    per = 3 if slices % 3 == 0 else 1
    half = (width if piece % 16 else width // 2, width)
    held = (slices, rows, width)
    enlarged, keep, send = at_once(
        functools.partial(absorb_kernel, n, n_sec, piece, per),
        "absorb",
        [
            jax.ShapeDtypeStruct(held, BF16),
            jax.ShapeDtypeStruct(half, F32),
            jax.ShapeDtypeStruct(half, BF16),
        ],
        [FAR, ARRAY, ARRAY],
        [
            pltpu.VMEM((n - 3, *held), BF16),
            pltpu.VMEM(held, BF16),
            pltpu.VMEM((width, width), F32),
            pltpu.SemaphoreType.DMA((n - 3, slices // per)),
            pltpu.SemaphoreType.DMA((slices // per,)),
        ],
        (me, counts),
        (c_parts, projectors, begun, e_far[-1]),
        tuple(e_far[:-1]),
        vmem=16 * 1024 * 1024,
    )
    if piece % 16:
        keep = relative(keep, me, n_sec, n_y)[0]
        send = relative(send, me, n_sec, n_y)[1]
    shape = (n_sec, n_y * piece, width)
    return enlarged, keep.reshape(shape), send.reshape(shape)


def relative(value, me, n_sec, n_y):
    rows, cols = value.shape
    value = value.reshape(2, n_sec, n_y, rows // (2 * n_sec * n_y), cols)
    value = jnp.take(value, jnp.arange(2) ^ (me[0] & 1), axis=0)
    value = jnp.take(value, jnp.arange(n_sec) ^ me[1], axis=1)
    return jnp.take(value, jnp.arange(n_y) ^ (me[0] >> 1), axis=2).reshape(2, rows // 2, cols)


class Order:
    def __init__(self):
        self.last = None

    def __call__(self, step, *args):
        if self.last is not None:
            args = lax.optimization_barrier((*args, self.last))[:-1]
        out = step(*args)
        self.last = jax.tree.leaves(out)[0]
        return out


def add_core(keep, arrived):
    total = keep + arrived.astype(F32)
    return total.astype(BF16), total[0]


def add_sec(total, *arrived):
    for block in arrived:
        total = total + block.astype(F32)
    total = total.reshape(lax.axis_size("env") // 2, -1, total.shape[-1])
    return total.astype(BF16), total[0]


def add_chips(total, *arrived):
    for block in arrived:
        total = total + block.astype(F32)
    return total.astype(BF16)


def join(*blocks):
    return jnp.concatenate(blocks, axis=0)


def to_sec(blocks):
    return [swap(blocks[m], "sec", m) for m in range(1, lax.axis_size("sec"))]


def to_chips(blocks):
    return [swap(blocks[m], "env", 2 * m) for m in range(1, lax.axis_size("env") // 2)]


def all_chips(block):
    return [block] + to_chips([block] * (lax.axis_size("env") // 2))


def all_sec(block):
    return [block] + to_sec([block] * lax.axis_size("sec"))


def gradient_kernel(n, n_sec, piece, per, slot, me, counts, *refs):
    blocks, refs = refs[: 2 * n_sec], refs[2 * n_sec :]
    p_ref, last_e, refs = refs[0], refs[1], refs[2:]
    cot_refs, far_refs, refs = refs[:n], refs[n : 2 * n - 1], refs[2 * n - 1 :]
    g_ref, own_ref, out, full, cot, held, grad, acc, sems, cot_sems = refs
    slices, rows, width = p_ref.shape
    cols = width // n_sec
    n_y = n // 2
    cot_copies = [
        pltpu.make_async_copy(cot_refs[m].at[slot], cot.at[m], cot_sems.at[m]) for m in range(n)
    ]
    for copy in cot_copies:
        copy.start()
    e_copies = [
        pltpu.make_async_copy(far_refs[m], held.at[m], sems.at[m]) for m in range(n - 1)
    ]
    for copy in e_copies:
        copy.start()
    e_refs = [*[held.at[m] for m in range(n - 1)], last_e]

    for m_core in range(2):
        for m_sec in range(n_sec):
            block = blocks[m_core * n_sec + m_sec]
            if piece % 16:
                at = (m_core * n_sec + m_sec) * n_y * piece
                full[at : at + n_y * piece] = block[...]
                continue
            for m_y in range(n_y):
                to = place(me, m_core, m_sec, m_y, n_sec, n_y, piece)
                full[pl.ds(to, piece), :] = block[m_y * piece : (m_y + 1) * piece]
    for copy in cot_copies:
        copy.wait()
    step = 16
    sums = (jnp.zeros((step, width), F32),) * 2

    def place_of(m, i):
        return pl.ds(pl.multiple_of((me[0] ^ m) * rows + i * step, step), step)

    def cot_of(m, i):
        return cot[m, pl.ds(pl.multiple_of(i * step, step), step), :].astype(F32)

    for m in range(n):

        def add(i, sums, m=m):
            x, c = full[place_of(m, i), :].astype(F32), cot_of(m, i)
            return sums[0] + x * x, sums[1] + c * x

        sums = lax.fori_loop(0, rows // step, add, sums, unroll=3)
    norm_sq = jnp.sum(sums[0], keepdims=True)
    cross = jnp.sum(sums[1], keepdims=True)
    scale = width / jnp.sqrt(norm_sq)
    ratio = scale * cross * scale / (width * width)
    for m in range(n):

        def write(i, _, m=m):
            x = full[place_of(m, i), :].astype(F32)
            g_ref[place_of(m, i), :] = (scale * (cot_of(m, i) - x * ratio)).astype(BF16)
            return _

        lax.fori_loop(0, rows // step, write, 0, unroll=3)
    own = full[pl.ds(pl.multiple_of(me[0] * rows, rows), rows), :]
    picked = own[:, :cols]
    for q in range(1, n_sec):
        picked = jnp.where(me[1] == q, own[:, q * cols : (q + 1) * cols], picked)
    own_ref[...] = picked.astype(F32) * scale

    for k in range(slices // per):
        x = dot(p_ref[k * per : k * per + per].reshape(per * rows, width), g_ref[...])
        for i in range(per):
            part = x[i * rows : (i + 1) * rows]
            keep = keep_columns(part.shape, 0, counts[k * per + i])
            grad[k * per + i] = jnp.where(keep, part, 0.0).astype(BF16)
    for copy in e_copies:
        copy.wait()
    for m in range(n):
        x = None
        for k in range(slices):
            y = dot(e_refs[m][k], grad[k], ((1,), (1,)))
            x = y if x is None else x + y
        acc[pl.ds(pl.multiple_of((me[0] ^ m) * rows, rows), rows), :] = x
    for m in range(n_sec):
        at = pl.multiple_of((me[1] ^ m) * cols, cols)
        out[m] = acc[pl.ds(at, cols), :].T.astype(BF16)


def gradient(me, counts, halves, cots, slot, projectors, e_blocks):
    slices, rows, width = projectors.shape
    n, n_sec, _, piece = sizes(rows, width)
    per = 3 if slices % 3 == 0 else 1
    cols = width // n_sec
    held = (slices, rows, width)
    return at_once(
        functools.partial(gradient_kernel, n, n_sec, piece, per, slot),
        "gradient",
        [
            jax.ShapeDtypeStruct((width, width), BF16),
            jax.ShapeDtypeStruct((rows, cols), F32),
            jax.ShapeDtypeStruct((n_sec, rows, cols), BF16),
        ],
        [ARRAY] * 3,
        [
            pltpu.VMEM((width, width), BF16),
            pltpu.VMEM((n, rows, width), BF16),
            pltpu.VMEM((n - 1, *held), BF16),
            pltpu.VMEM(held, BF16),
            pltpu.VMEM((width, rows), F32),
            pltpu.SemaphoreType.DMA((n - 1,)),
            pltpu.SemaphoreType.DMA((n,)),
        ],
        (me, counts),
        (*halves, projectors, e_blocks[-1]),
        (*cots, *e_blocks[:-1]),
        vmem=24 * 1024 * 1024,
        nbytes=20 * slices * rows * width,
    )


def early_kernel(per, first, counts, g_ref, enl_ref, q_ref, *refs):
    proj, edge = refs[-2:]
    k = pl.program_id(0)
    for i in range(per):
        proj[i] = dot(enl_ref[i], g_ref[...], ((1,), (1,)))
    x = dot(q_ref[0], g_ref[...])
    edge[0] = jnp.where(keep_columns(x.shape, 0, counts[first + k]), x, 0.0)


def early_gradients(results, counts, g, enlarged, q, first, steps):
    slices, rows, width = enlarged.shape
    per = 3 if slices % 3 == 0 else 1
    last = q.shape[0] - 1
    out = jax.ShapeDtypeStruct((slices, rows, width), F32)
    return pl.pallas_call(
        functools.partial(early_kernel, per, first),
        grid_spec=pltpu.PrefetchScalarGridSpec(
            num_scalar_prefetch=1,
            grid=(steps,),
            in_specs=[
                whole((width, width)),
                group(per, (rows, width), 0, first),
                pl.BlockSpec((1, rows, width), lambda k, *s: (jnp.minimum(k + first, last), 0, 0)),
            ]
            + [FAR] * len(results),
            out_specs=[group(per, (rows, width), 0, first), group(1, (rows, width), 0, first)],
        ),
        out_shape=[out, out],
        input_output_aliases={4 + j: j for j in range(len(results))},
        name="early_gradients",
        compiler_params=pltpu.CompilerParams(vmem_limit_bytes=24 * 1024 * 1024),
        cost_estimate=pl.CostEstimate(flops=1000, bytes_accessed=1000, transcendentals=0),
    )(counts, g, enlarged, q, *results)


def finish(n, across, begun, p_refs, i):
    y = begun[i]
    for m in range(n - 2):
        y = y + dot(across[m], p_refs[m][i])
    return y.astype(BF16)


def mix_kernel(n, slices, c_ref, begun, *refs):
    across = [c_ref[m].T for m in range(n - 2)]
    for i in range(slices):
        refs[-1][i] = finish(n, across, begun, refs, i)


def mix(c_far, begun, p_far):
    slices, rows, width = begun.shape
    return call(
        functools.partial(mix_kernel, c_far.shape[0] + 2, slices),
        "mix",
        (1,),
        [whole(c_far.shape)] + [group(slices, (rows, width))] * (1 + len(p_far)),
        group(slices, (rows, width)),
        jax.ShapeDtypeStruct((slices, rows, width), BF16),
        [],
        0,
        0,
        0,
        (c_far, begun, *p_far),
    )


def spans(slices, per):
    return [(at, min(per, slices - at)) for at in range(0, slices, per)]


def late_kernel(n, first, groups, counts, g_ref, c_ref, fwd, *refs):
    far_refs, refs = refs[: n - 2], refs[n - 2 :]
    _, out, begun, held, q, x, sems, out_sems = refs
    slices, rows, width = begun.shape
    buffers = [begun, *[held.at[m] for m in range(n - 3)]]
    copies, stores = [], []
    for k, (at, size) in enumerate(groups):
        at = pl.ds(at, size)
        copies.append([
            pltpu.make_async_copy(far_refs[j].at[at], buffers[j].at[at], sems.at[j, k])
            for j in range(n - 2)
        ])
        for copy in copies[-1]:
            copy.start()
    across = [c_ref[m].T for m in range(n - 2)]
    p_refs = [*buffers[1:], fwd]
    for k, (at, size) in enumerate(groups):
        for copy in copies[k]:
            copy.wait()
        for i in range(size):
            q[i * rows : (i + 1) * rows] = finish(n, across, begun, p_refs, at + i)
        y = dot(q[: size * rows], g_ref[...])
        for i in range(size):
            part = y[i * rows : (i + 1) * rows]
            keep = keep_columns(part.shape, 0, counts[first + at + i])
            x[at + i] = jnp.where(keep, part, 0.0)
        to = out.at[pl.ds(first + at, size)]
        stores.append(pltpu.make_async_copy(x.at[pl.ds(at, size)], to, out_sems.at[k]))
        stores[-1].start()
    for store in stores:
        store.wait()


def late_edge_gradient(result, counts, g, c_far, begun, p_far, first):
    n = c_far.shape[0] + 2
    slices, rows, width = begun.shape
    groups = spans(slices, 2)
    return at_once(
        functools.partial(late_kernel, n, first, groups),
        "late_edge_gradient",
        jax.ShapeDtypeStruct(result.shape, F32),
        FAR,
        [
            pltpu.VMEM((slices, rows, width), F32),
            pltpu.VMEM((n - 3, slices, rows, width), BF16),
            pltpu.VMEM((2 * rows, width), BF16),
            pltpu.VMEM((slices, rows, width), F32),
            pltpu.SemaphoreType.DMA((n - 2, len(groups))),
            pltpu.SemaphoreType.DMA((len(groups),)),
        ],
        (counts,),
        (g, c_far, p_far[-1]),
        (begun, *p_far[:-1], result),
        {4 + n - 2: 0},
        vmem=48 * 1024 * 1024,
    )


def cotangent_order(*blocks):
    n_sec, s = lax.axis_size("sec"), lax.axis_index("sec")
    ordered = []
    for q in range(n_sec):
        block = blocks[0]
        for m in range(1, n_sec):
            block = jnp.where((s ^ m) == q, blocks[m], block)
        ordered.append(block)
    return jnp.concatenate(ordered, axis=1)


def per_device(corner, edges, projectors, tile_counts, cotangent):
    n, n_sec = lax.axis_size("env"), lax.axis_size("sec")
    e, s = lax.axis_index("env"), lax.axis_index("sec")
    slices, rows, width = edges.shape
    cols = cotangent.shape[1]
    piece = width // (n * n_sec)
    me = jnp.stack([e, s]).astype(jnp.int32)
    core, y = e & 1, e >> 1

    def from_chips(value):
        return to_chips([value] * (n // 2))

    def both_cores(arrived):
        return [b for block in arrived for b in (block, swap(block, "env", 1))]

    def barrier(value, *earlier):
        return lax.optimization_barrier((value, earlier))[0]

    far = from_chips(edges)
    cot = cotangent.astype(BF16)
    cot = cotangent_order(cot, *to_sec([cot] * n_sec))
    early = max(slices // 3, 1)
    pieces = [
        jnp.concatenate([projectors[:early], corner[None], cot[None]], axis=0),
        projectors[early:],
    ]
    near = [swap(p, "env", 1) for p in pieces]
    c_parts = jnp.stack(
        [lax.dynamic_slice_in_dim(corner, (e ^ m) * rows, rows, 1) for m in range(n)]
    )
    e_near = swap(edges, "env", 1)
    begun = begin(c_parts, edges, e_near)

    def corner_columns(piece):
        return lax.dynamic_slice_in_dim(piece[early], e * rows, rows, 1)

    c_near = jnp.stack([corner_columns(pieces[0]).T, corner_columns(near[0]).T])
    mixing = [begin(c_near, p, q) for p, q in zip(pieces, near)]
    mixing[0] = mixing[0][:early]
    far = barrier(far, begun, mixing)
    p_far = [from_chips(barrier(pieces[0], far))]
    e_blocks = [edges, e_near, *both_cores(far)]

    order = Order()

    enlarged, keep, send = order(
        lambda *f: absorb(me, tile_counts, c_parts, begun, f, projectors), *e_blocks[2:])
    moved, total = order(add_core, keep, swap(send, "env", 1))
    sec = to_sec(moved)
    total = barrier(total, p_far[0])
    moved, total = order(add_sec, total, *sec)
    own = order(add_chips, total, *to_chips(moved))
    some = order(join, *all_chips(own))
    half = all_sec(some)
    p_far += [from_chips(barrier(p, some)) for p in pieces[1:]]
    p_far[0] = both_cores(barrier(p_far[0], some))
    cots = [pieces[0], near[0], *p_far[0]]
    c_far = jnp.stack([corner_columns(p) for p in p_far[0]])
    q = order(lambda c: mix(c, mixing[0], p_far[0]), c_far)
    half = barrier(half, order.last)
    halves = half + [swap(h, "env", 1) for h in half]
    if piece % 16:
        halves = list(
            relative(jnp.concatenate(halves), me, n_sec, n // 2).reshape(2 * n_sec, -1, width))
    g, corner_new, part = order(
        lambda *h: gradient(me, tile_counts, h, cots, early + 1, projectors, e_blocks), *halves)
    moved = to_sec(part)
    steps = slices // 3 if slices % 3 == 0 else slices
    some_steps = max(steps - 1, 1)
    results = order(
        lambda g: early_gradients((), tile_counts, g, enlarged, q, 0, some_steps), g)
    corner_grad = order(
        lambda *b: sum((x.astype(F32) for x in b[1:]), b[0].astype(F32)), part[0], *moved)
    p_far = both_cores(barrier(p_far[1], corner_grad))
    proj_grad, edge_grad = order(
        lambda *r: early_gradients(
            r, tile_counts, g, enlarged, q, some_steps, steps - some_steps), *results)
    edge_grad = order(
        lambda r, *p: late_edge_gradient(r, tile_counts, g, c_far, mixing[1], p, early),
        edge_grad, *p_far)
    return (corner_new, corner_grad, edge_grad, proj_grad)


def solution(mesh):
    placed = (
        P(("sweep", "env"), None),
        P(("sweep", "sec"), "env", None),
        P(("sweep", "sec"), "env", None),
        P(("sweep", "sec")),
        P(("sweep", "env"), "sec"),
    )
    return jax.shard_map(
        per_device,
        mesh=mesh,
        in_specs=placed,
        out_specs=(
            P(("sweep", "env"), "sec"),
            P(("sweep", "env"), "sec"),
            P(("sweep", "sec"), "env", None),
            P(("sweep", "sec"), "env", None),
        ),
        check_vma=False,
    )
```

```python
import functools

import jax
import jax.numpy as jnp
from jax import lax
from jax.experimental import pallas as pl
from jax.experimental.pallas import tpu as pltpu
from jax.sharding import PartitionSpec as P

TILE = 128
F32, BF16 = jnp.float32, jnp.bfloat16
VMEM_LIMIT = 40 * 1024 * 1024


def swap(value, axis, offset):
    size = lax.axis_size(axis)
    return lax.ppermute(value, axis, [(i, i ^ offset) for i in range(size)])


def after(value, *earlier):
    return lax.optimization_barrier((value, *earlier))[0]


def dot(a, b, dims=((1,), (0,))):
    return lax.dot_general(a, b, (dims, ((), ())), preferred_element_type=F32)


def call(kernel, name, grid, in_specs, out_specs, out_shape, scratch, flops, nbytes, prefetch, args):
    return pl.pallas_call(
        kernel,
        grid_spec=pltpu.PrefetchScalarGridSpec(
            num_scalar_prefetch=prefetch,
            grid=grid,
            in_specs=in_specs,
            out_specs=out_specs,
            scratch_shapes=scratch,
        ),
        out_shape=out_shape,
        name=name,
        compiler_params=pltpu.CompilerParams(vmem_limit_bytes=VMEM_LIMIT),
        cost_estimate=pl.CostEstimate(flops=1000, bytes_accessed=1000, transcendentals=0),
    )(*args)


def keep_columns(shape, first, count):
    return lax.broadcasted_iota(jnp.int32, shape, 1) + first < count * TILE


def whole(shape):
    return pl.BlockSpec(shape, lambda k, *s: (0,) * len(shape))


def group(size, shape, column=0, first=0):
    return pl.BlockSpec((size, *shape), lambda k, *s: (k + first, 0, column))


def sizes(mesh_rows, width):
    n, n_sec = lax.axis_size("env"), lax.axis_size("sec")
    return n, n_sec, n // 2, width // (n * n_sec)


def place(me, m_core, m_sec, m_y, n_sec, n_y, piece):
    core, y = me[0] & 1, me[0] >> 1
    at = (((core ^ m_core) * n_sec + (me[1] ^ m_sec)) * n_y + (y ^ m_y)) * piece
    return pl.multiple_of(at, piece)


def fetch(per, ref, buffer, rows, sems):
    copies = []
    for k in range(ref.shape[0] // per):
        at = pl.ds(k * per, per)
        copies.append(pltpu.make_async_copy(ref.at[at], buffer.at[at, rows], sems.at[k]))
        copies[-1].start()
    return copies


def begin_kernel(per, c_ref, own, near, out):
    for i in range(per):
        out[i] = dot(c_ref[0], own[i]) + dot(c_ref[1], near[i])


def begin(c_parts, own, near):
    slices, rows, width = own.shape
    per = 3 if slices % 3 == 0 else 1
    return call(
        functools.partial(begin_kernel, per),
        "begin",
        (slices // per,),
        [whole(c_parts.shape)] + [group(per, (rows, width))] * 2,
        group(per, (c_parts.shape[1], width)),
        jax.ShapeDtypeStruct((slices, c_parts.shape[1], width), F32),
        [],
        0,
        0,
        0,
        (c_parts, own, near),
    )


def absorb_kernel(n, n_sec, piece, per, me, counts, c_ref, p_ref, begun, fwd, *refs):
    far_refs, (enl_ref, keep_ref, send_ref, held, enl, acc, sems, out_sems) = refs[:-8], refs[-8:]
    n_y = n // 2
    slices, rows, width = p_ref.shape
    copies = [
        fetch(per, far_refs[m], held.at[m], pl.ds(0, rows), sems.at[m]) for m in range(n - 3)
    ]
    stores = []
    for k in range(slices // per):
        at = pl.ds(k * per, per)
        for m in range(n - 3):
            copies[m][k].wait()
        for i in range(k * per, k * per + per):
            x = begun[i] + dot(c_ref[n - 1], fwd[i])
            for m in range(n - 3):
                x = x + dot(c_ref[2 + m], held[m, i])
            enl[i] = jnp.where(keep_columns(x.shape, 0, counts[i]), x, 0.0).astype(BF16)
        stores.append(pltpu.make_async_copy(enl.at[at], enl_ref.at[at], out_sems.at[k]))
        stores[-1].start()
    half = width // 2
    for first in (0, half):
        acc[first : first + half, :] = dot(
            p_ref[:, :, first : first + half].reshape(slices * rows, half),
            enl[...].reshape(slices * rows, width),
            ((0,), (0,)),
        )
    if piece % 16:
        keep_ref[...] = acc[...]
        send_ref[...] = acc[...].astype(BF16)
    else:
        for m_sec in range(n_sec):
            for m_y in range(n_y):
                at = (m_sec * n_y + m_y) * piece
                for m_core, ref in ((0, keep_ref), (1, send_ref)):
                    part = acc[pl.ds(place(me, m_core, m_sec, m_y, n_sec, n_y, piece), piece), :]
                    ref[at : at + piece] = part.astype(ref.dtype)
    for store in stores:
        store.wait()


SCALARS = pl.BlockSpec(memory_space=pltpu.SMEM)
ARRAY = pl.BlockSpec(memory_space=pltpu.VMEM)
FAR = pl.BlockSpec(memory_space=pl.ANY)


def at_once(
    kernel, name, out_shape, out_specs, scratch, scalars, near, far, aliases=None, vmem=VMEM_LIMIT, nbytes=1000
):
    return pl.pallas_call(
        kernel,
        in_specs=[SCALARS] * len(scalars) + [ARRAY] * len(near) + [FAR] * len(far),
        out_specs=out_specs,
        out_shape=out_shape,
        scratch_shapes=scratch,
        input_output_aliases=aliases or {},
        name=name,
        compiler_params=pltpu.CompilerParams(vmem_limit_bytes=vmem),
        cost_estimate=pl.CostEstimate(flops=1000, bytes_accessed=nbytes, transcendentals=0),
    )(*scalars, *near, *far)


def absorb(me, counts, c_parts, begun, e_far, projectors):
    slices, rows, width = projectors.shape
    n, n_sec, n_y, piece = sizes(rows, width)
    per = 3 if slices % 3 == 0 else 1
    half = (width if piece % 16 else width // 2, width)
    held = (slices, rows, width)
    enlarged, keep, send = at_once(
        functools.partial(absorb_kernel, n, n_sec, piece, per),
        "absorb",
        [
            jax.ShapeDtypeStruct(held, BF16),
            jax.ShapeDtypeStruct(half, F32),
            jax.ShapeDtypeStruct(half, BF16),
        ],
        [FAR, ARRAY, ARRAY],
        [
            pltpu.VMEM((n - 3, *held), BF16),
            pltpu.VMEM(held, BF16),
            pltpu.VMEM((width, width), F32),
            pltpu.SemaphoreType.DMA((n - 3, slices // per)),
            pltpu.SemaphoreType.DMA((slices // per,)),
        ],
        (me, counts),
        (c_parts, projectors, begun, e_far[-1]),
        tuple(e_far[:-1]),
        vmem=16 * 1024 * 1024,
    )
    if piece % 16:
        keep = relative(keep, me, n_sec, n_y)[0]
        send = relative(send, me, n_sec, n_y)[1]
    shape = (n_sec, n_y * piece, width)
    return enlarged, keep.reshape(shape), send.reshape(shape)


def relative(value, me, n_sec, n_y):
    rows, cols = value.shape
    value = value.reshape(2, n_sec, n_y, rows // (2 * n_sec * n_y), cols)
    value = jnp.take(value, jnp.arange(2) ^ (me[0] & 1), axis=0)
    value = jnp.take(value, jnp.arange(n_sec) ^ me[1], axis=1)
    return jnp.take(value, jnp.arange(n_y) ^ (me[0] >> 1), axis=2).reshape(2, rows // 2, cols)


class Order:
    def __init__(self):
        self.last = None

    def __call__(self, step, *args):
        if self.last is not None:
            args = lax.optimization_barrier((*args, self.last))[:-1]
        out = step(*args)
        self.last = jax.tree.leaves(out)[0]
        return out


def add_core(keep, arrived):
    total = keep + arrived.astype(F32)
    return total.astype(BF16), total[0]


def add_sec(total, *arrived):
    for block in arrived:
        total = total + block.astype(F32)
    return total.astype(BF16)


def add_chips(own, *arrived):
    n_y = len(arrived) + 1
    total = own.astype(F32)
    for m, block in enumerate(arrived, 1):
        pieces = block.reshape(n_y, -1, block.shape[-1])
        block = jnp.concatenate([pieces[j ^ m] for j in range(n_y)], axis=0)
        total = total + block.astype(F32)
    return total.astype(BF16)


def to_sec(blocks):
    return [swap(blocks[m], "sec", m) for m in range(1, lax.axis_size("sec"))]


def to_chips(blocks):
    return [swap(blocks[m], "env", 2 * m) for m in range(1, lax.axis_size("env") // 2)]


def all_sec(block):
    return [block] + to_sec([block] * lax.axis_size("sec"))


def gradient_kernel(n, n_sec, piece, per, slot, me, counts, *refs):
    blocks, refs = refs[: 2 * n_sec], refs[2 * n_sec :]
    p_ref, last_e, refs = refs[0], refs[1], refs[2:]
    cot_refs, far_refs, refs = refs[:n], refs[n : 2 * n - 1], refs[2 * n - 1 :]
    g_ref, own_ref, out, full, cot, held, grad, acc, sems, cot_sems = refs
    slices, rows, width = p_ref.shape
    cols = width // n_sec
    n_y = n // 2
    cot_copies = [
        pltpu.make_async_copy(cot_refs[m].at[slot], cot.at[m], cot_sems.at[m]) for m in range(n)
    ]
    for copy in cot_copies:
        copy.start()
    e_copies = [
        pltpu.make_async_copy(far_refs[m], held.at[m], sems.at[m]) for m in range(n - 1)
    ]
    for copy in e_copies:
        copy.start()
    e_refs = [*[held.at[m] for m in range(n - 1)], last_e]

    for m_core in range(2):
        for m_sec in range(n_sec):
            block = blocks[m_core * n_sec + m_sec]
            if piece % 16:
                at = (m_core * n_sec + m_sec) * n_y * piece
                full[at : at + n_y * piece] = block[...]
                continue
            for m_y in range(n_y):
                to = place(me, m_core, m_sec, m_y, n_sec, n_y, piece)
                full[pl.ds(to, piece), :] = block[m_y * piece : (m_y + 1) * piece]
    for copy in cot_copies:
        copy.wait()
    step = 16
    sums = (jnp.zeros((step, width), F32),) * 2

    def place_of(m, i):
        return pl.ds(pl.multiple_of((me[0] ^ m) * rows + i * step, step), step)

    def cot_of(m, i):
        return cot[m, pl.ds(pl.multiple_of(i * step, step), step), :].astype(F32)

    for m in range(n):

        def add(i, sums, m=m):
            x, c = full[place_of(m, i), :].astype(F32), cot_of(m, i)
            return sums[0] + x * x, sums[1] + c * x

        sums = lax.fori_loop(0, rows // step, add, sums, unroll=3)
    norm_sq = jnp.sum(sums[0], keepdims=True)
    cross = jnp.sum(sums[1], keepdims=True)
    scale = width / jnp.sqrt(norm_sq)
    ratio = scale * cross * scale / (width * width)
    for m in range(n):

        def write(i, _, m=m):
            x = full[place_of(m, i), :].astype(F32)
            g_ref[place_of(m, i), :] = (scale * (cot_of(m, i) - x * ratio)).astype(BF16)
            return _

        lax.fori_loop(0, rows // step, write, 0, unroll=3)
    own = full[pl.ds(pl.multiple_of(me[0] * rows, rows), rows), :]
    picked = own[:, :cols]
    for q in range(1, n_sec):
        picked = jnp.where(me[1] == q, own[:, q * cols : (q + 1) * cols], picked)
    own_ref[...] = picked.astype(F32) * scale

    for k in range(slices // per):
        x = dot(p_ref[k * per : k * per + per].reshape(per * rows, width), g_ref[...])
        for i in range(per):
            part = x[i * rows : (i + 1) * rows]
            keep = keep_columns(part.shape, 0, counts[k * per + i])
            grad[k * per + i] = jnp.where(keep, part, 0.0).astype(BF16)
    for copy in e_copies:
        copy.wait()
    for m in range(n):
        x = None
        for k in range(slices):
            y = dot(e_refs[m][k], grad[k], ((1,), (1,)))
            x = y if x is None else x + y
        acc[pl.ds(pl.multiple_of((me[0] ^ m) * rows, rows), rows), :] = x
    for m in range(n_sec):
        at = pl.multiple_of((me[1] ^ m) * cols, cols)
        out[m] = acc[pl.ds(at, cols), :].astype(BF16).T


def gradient(me, counts, halves, cots, slot, projectors, e_blocks):
    slices, rows, width = projectors.shape
    n, n_sec, _, piece = sizes(rows, width)
    per = 3 if slices % 3 == 0 else 1
    cols = width // n_sec
    held = (slices, rows, width)
    return at_once(
        functools.partial(gradient_kernel, n, n_sec, piece, per, slot),
        "gradient",
        [
            jax.ShapeDtypeStruct((width, width), BF16),
            jax.ShapeDtypeStruct((rows, cols), F32),
            jax.ShapeDtypeStruct((n_sec, rows, cols), BF16),
        ],
        [ARRAY] * 3,
        [
            pltpu.VMEM((width, width), BF16),
            pltpu.VMEM((n, rows, width), BF16),
            pltpu.VMEM((n - 1, *held), BF16),
            pltpu.VMEM(held, BF16),
            pltpu.VMEM((width, rows), F32),
            pltpu.SemaphoreType.DMA((n - 1,)),
            pltpu.SemaphoreType.DMA((n,)),
        ],
        (me, counts),
        (*halves, projectors, e_blocks[-1]),
        (*cots, *e_blocks[:-1]),
        vmem=24 * 1024 * 1024,
        nbytes=20 * slices * rows * width,
    )


def outputs_kernel(per, dims, counts, g_ref, x_ref, out, held, sems):
    slices, rows, width = x_ref.shape
    stores = []
    for k in range(slices // per):
        at = pl.ds(k * per, per)
        y = dot(x_ref[k * per : k * per + per].reshape(per * rows, width), g_ref[...], dims)
        for i in range(per):
            part = y[i * rows : (i + 1) * rows]
            if dims[1] == (0,):
                keep = keep_columns(part.shape, 0, counts[k * per + i])
                part = jnp.where(keep, part, 0.0)
            held[k * per + i] = part
        stores.append(pltpu.make_async_copy(held.at[at], out.at[at], sems.at[k]))
        stores[-1].start()
    for copy in stores:
        copy.wait()


def outputs(name, counts, g, x, slices, dims):
    count, rows, width = x.shape
    per = 3 if count % 3 == 0 else 1
    return at_once(
        functools.partial(outputs_kernel, per, dims),
        name,
        jax.ShapeDtypeStruct((slices, rows, width), F32),
        FAR,
        [pltpu.VMEM((count, rows, width), F32), pltpu.SemaphoreType.DMA((count // per,))],
        (counts,),
        (g, x),
        (),
        vmem=24 * 1024 * 1024,
    )


def finish(n, across, begun, p_refs, i):
    y = begun[i]
    for m in range(n - 2):
        y = y + dot(across[m], p_refs[m][i])
    return y.astype(BF16)


def mix_kernel(n, slices, c_ref, begun, *refs):
    across = [c_ref[m].T for m in range(n - 2)]
    for i in range(slices):
        refs[-1][i] = finish(n, across, begun, refs, i)


def mix(c_far, begun, p_far):
    slices, rows, width = begun.shape
    return call(
        functools.partial(mix_kernel, c_far.shape[0] + 2, slices),
        "mix",
        (1,),
        [whole(c_far.shape)] + [group(slices, (rows, width))] * (1 + len(p_far)),
        group(slices, (rows, width)),
        jax.ShapeDtypeStruct((slices, rows, width), BF16),
        [],
        0,
        0,
        0,
        (c_far, begun, *p_far),
    )


def spans(slices, per):
    return [(at, min(per, slices - at)) for at in range(0, slices, per)]


def add_far_kernel(n, per, c_ref, begun, *refs):
    across = [c_ref[m].T for m in range(n - 3)]
    for i in range(per):
        y = begun[i]
        for m in range(n - 3):
            y = y + dot(across[m], refs[m][i])
        refs[-1][i] = y


def add_far(c_far, begun, far):
    slices, rows, width = begun.shape
    n = c_far.shape[0] + 2
    per = 3 if slices % 3 == 0 else 1
    return call(
        functools.partial(add_far_kernel, n, per),
        "add_far",
        (slices // per,),
        [whole(c_far.shape)] + [group(per, (rows, width))] * (n - 2),
        group(per, (rows, width)),
        jax.ShapeDtypeStruct((slices, rows, width), F32),
        [],
        0,
        0,
        0,
        (c_far, begun, *far),
    )


def late_kernel(first, groups, counts, g_ref, c_ref, begun, fwd, _, out, q, x, out_sems):
    slices, rows, width = begun.shape
    across = c_ref[...].T
    stores = []
    for k, (at, size) in enumerate(groups):
        for i in range(size):
            y = begun[at + i] + dot(across, fwd[at + i])
            q[i * rows : (i + 1) * rows] = y.astype(BF16)
        y = dot(q[: size * rows], g_ref[...])
        for i in range(size):
            part = y[i * rows : (i + 1) * rows]
            keep = keep_columns(part.shape, 0, counts[first + at + i])
            x[at + i] = jnp.where(keep, part, 0.0)
        to = out.at[pl.ds(first + at, size)]
        stores.append(pltpu.make_async_copy(x.at[pl.ds(at, size)], to, out_sems.at[k]))
        stores[-1].start()
    for store in stores:
        store.wait()


def late_edge_gradient(result, counts, g, c_last, begun, fwd, first):
    slices, rows, width = begun.shape
    groups = spans(slices, 2)
    return at_once(
        functools.partial(late_kernel, first, groups),
        "late_edge_gradient",
        jax.ShapeDtypeStruct(result.shape, F32),
        FAR,
        [
            pltpu.VMEM((2 * rows, width), BF16),
            pltpu.VMEM((slices, rows, width), F32),
            pltpu.SemaphoreType.DMA((len(groups),)),
        ],
        (counts,),
        (g, c_last, begun, fwd),
        (result,),
        {5: 0},
        vmem=16 * 1024 * 1024,
    )


def cotangent_order(*blocks):
    n_sec, s = lax.axis_size("sec"), lax.axis_index("sec")
    ordered = []
    for q in range(n_sec):
        block = blocks[0]
        for m in range(1, n_sec):
            block = jnp.where((s ^ m) == q, blocks[m], block)
        ordered.append(block)
    return jnp.concatenate(ordered, axis=1)


def per_device(corner, edges, projectors, tile_counts, cotangent):
    n, n_sec = lax.axis_size("env"), lax.axis_size("sec")
    e, s = lax.axis_index("env"), lax.axis_index("sec")
    slices, rows, width = edges.shape
    cols = cotangent.shape[1]
    piece = width // (n * n_sec)
    me = jnp.stack([e, s]).astype(jnp.int32)
    core, y = e & 1, e >> 1

    def from_chips(value):
        return to_chips([value] * (n // 2))

    def both_cores(arrived):
        return [b for block in arrived for b in (block, swap(block, "env", 1))]

    def barrier(value, *earlier):
        return lax.optimization_barrier((value, earlier))[0]

    far = from_chips(edges)
    cot = cotangent.astype(BF16)
    cot = cotangent_order(cot, *to_sec([cot] * n_sec))
    early = max(slices // 3, 1)
    pieces = [
        jnp.concatenate([projectors[:early], corner[None], cot[None]], axis=0),
        projectors[early:],
    ]
    near = [swap(p, "env", 1) for p in pieces]
    c_parts = jnp.stack(
        [lax.dynamic_slice_in_dim(corner, (e ^ m) * rows, rows, 1) for m in range(n)]
    )
    e_near = swap(edges, "env", 1)
    begun = begin(c_parts, edges, e_near)

    def corner_columns(piece):
        return lax.dynamic_slice_in_dim(piece[early], e * rows, rows, 1)

    c_near = jnp.stack([corner_columns(pieces[0]).T, corner_columns(near[0]).T])
    mixing = [begin(c_near, p, q) for p, q in zip(pieces, near)]
    mixing[0] = mixing[0][:early]
    far = barrier(far, begun, mixing)
    p_far = [from_chips(pieces[0])]
    e_blocks = [edges, e_near, *both_cores(far)]

    order = Order()

    enlarged, keep, send = order(
        lambda *f: absorb(me, tile_counts, c_parts, begun, f, projectors), *e_blocks[2:])
    moved, total = order(add_core, keep, swap(send, "env", 1))
    sec = to_sec(moved)
    total = barrier(total, p_far[0])
    some = order(add_sec, total, *sec)
    some = order(add_chips, some, *from_chips(some))
    half = all_sec(some)
    p_far += [from_chips(barrier(p, some)) for p in pieces[1:]]
    p_far[0] = both_cores(barrier(p_far[0], some))
    cots = [pieces[0], near[0], *p_far[0]]
    c_far = jnp.stack([corner_columns(p) for p in p_far[0]])
    q = order(lambda c: mix(c, mixing[0], p_far[0]), c_far)
    half = barrier(half, order.last)
    halves = half + [swap(h, "env", 1) for h in half]
    if piece % 16:
        halves = list(
            relative(jnp.concatenate(halves), me, n_sec, n // 2).reshape(2 * n_sec, -1, width))
    g, corner_new, part = order(
        lambda *h: gradient(me, tile_counts, h, cots, early + 1, projectors, e_blocks), *halves)
    moved = to_sec(part)
    proj_grad = order(
        lambda g: outputs(
            "proj_gradient", tile_counts, g, enlarged, slices, ((1,), (1,))), g)
    edge_grad = order(
        lambda g: outputs("edge_gradient", tile_counts, g, q, slices, ((1,), (0,))), g)
    corner_grad = order(
        lambda *b: sum((x.astype(F32) for x in b[1:]), b[0].astype(F32)), part[0], *moved)
    p_far = both_cores(barrier(p_far[1], corner_grad))
    begun = order(lambda b, *p: add_far(c_far, b, p), mixing[1], *p_far[:-1])
    edge_grad = order(
        lambda r, b, p: late_edge_gradient(r, tile_counts, g, c_far[-1], b, p, early),
        edge_grad, begun, p_far[-1])
    return (corner_new, corner_grad, edge_grad, proj_grad)


def solution(mesh):
    placed = (
        P(("sweep", "env"), None),
        P(("sweep", "sec"), "env", None),
        P(("sweep", "sec"), "env", None),
        P(("sweep", "sec")),
        P(("sweep", "env"), "sec"),
    )
    return jax.shard_map(
        per_device,
        mesh=mesh,
        in_specs=placed,
        out_specs=(
            P(("sweep", "env"), "sec"),
            P(("sweep", "env"), "sec"),
            P(("sweep", "sec"), "env", None),
            P(("sweep", "sec"), "env", None),
        ),
        check_vma=False,
    )
```

```python
import functools

import jax
import jax.numpy as jnp
from jax import lax
from jax.experimental import pallas as pl
from jax.experimental.pallas import tpu as pltpu
from jax.sharding import PartitionSpec as P

TILE = 128
F32, BF16 = jnp.float32, jnp.bfloat16
VMEM_LIMIT = 40 * 1024 * 1024


def swap(value, axis, offset):
    size = lax.axis_size(axis)
    return lax.ppermute(value, axis, [(i, i ^ offset) for i in range(size)])


def after(value, *earlier):
    return lax.optimization_barrier((value, *earlier))[0]


def dot(a, b, dims=((1,), (0,))):
    return lax.dot_general(a, b, (dims, ((), ())), preferred_element_type=F32)


def call(kernel, name, grid, in_specs, out_specs, out_shape, scratch, flops, nbytes, prefetch, args):
    return pl.pallas_call(
        kernel,
        grid_spec=pltpu.PrefetchScalarGridSpec(
            num_scalar_prefetch=prefetch,
            grid=grid,
            in_specs=in_specs,
            out_specs=out_specs,
            scratch_shapes=scratch,
        ),
        out_shape=out_shape,
        name=name,
        compiler_params=pltpu.CompilerParams(vmem_limit_bytes=VMEM_LIMIT),
        cost_estimate=pl.CostEstimate(flops=1000, bytes_accessed=1000, transcendentals=0),
    )(*args)


def keep_columns(shape, first, count):
    return lax.broadcasted_iota(jnp.int32, shape, 1) + first < count * TILE


def whole(shape):
    return pl.BlockSpec(shape, lambda k, *s: (0,) * len(shape))


def group(size, shape, column=0, first=0):
    return pl.BlockSpec((size, *shape), lambda k, *s: (k + first, 0, column))


def sizes(mesh_rows, width):
    n, n_sec = lax.axis_size("env"), lax.axis_size("sec")
    return n, n_sec, n // 2, width // (n * n_sec)


def place(me, m_core, m_sec, m_y, n_sec, n_y, piece):
    core, y = me[0] & 1, me[0] >> 1
    at = (((core ^ m_core) * n_sec + (me[1] ^ m_sec)) * n_y + (y ^ m_y)) * piece
    return pl.multiple_of(at, piece)


def fetch(per, ref, buffer, rows, sems):
    copies = []
    for k in range(ref.shape[0] // per):
        at = pl.ds(k * per, per)
        copies.append(pltpu.make_async_copy(ref.at[at], buffer.at[at, rows], sems.at[k]))
        copies[-1].start()
    return copies


def begin_kernel(per, c_ref, own, near, out):
    for i in range(per):
        out[i] = dot(c_ref[0], own[i]) + dot(c_ref[1], near[i])


def begin(c_parts, own, near):
    slices, rows, width = own.shape
    per = 3 if slices % 3 == 0 else 1
    return call(
        functools.partial(begin_kernel, per),
        "begin",
        (slices // per,),
        [whole(c_parts.shape)] + [group(per, (rows, width))] * 2,
        group(per, (c_parts.shape[1], width)),
        jax.ShapeDtypeStruct((slices, c_parts.shape[1], width), F32),
        [],
        0,
        0,
        0,
        (c_parts, own, near),
    )


def absorb_kernel(n, n_sec, piece, per, me, counts, c_ref, p_ref, begun, fwd, *refs):
    far_refs, (enl_ref, keep_ref, send_ref, held, enl, acc, sems, out_sems) = refs[:-8], refs[-8:]
    n_y = n // 2
    slices, rows, width = p_ref.shape
    copies = [
        fetch(per, far_refs[m], held.at[m], pl.ds(0, rows), sems.at[m]) for m in range(n - 3)
    ]
    stores = []
    for k in range(slices // per):
        at = pl.ds(k * per, per)
        for m in range(n - 3):
            copies[m][k].wait()
        for i in range(k * per, k * per + per):
            x = begun[i] + dot(c_ref[n - 1], fwd[i])
            for m in range(n - 3):
                x = x + dot(c_ref[2 + m], held[m, i])
            enl[i] = jnp.where(keep_columns(x.shape, 0, counts[i]), x, 0.0).astype(BF16)
        stores.append(pltpu.make_async_copy(enl.at[at], enl_ref.at[at], out_sems.at[k]))
        stores[-1].start()
    half = width // 2
    for first in (0, half):
        acc[first : first + half, :] = dot(
            p_ref[:, :, first : first + half].reshape(slices * rows, half),
            enl[...].reshape(slices * rows, width),
            ((0,), (0,)),
        )
    if piece % 16:
        keep_ref[...] = acc[...]
        send_ref[...] = acc[...].astype(BF16)
    else:
        for m_sec in range(n_sec):
            for m_y in range(n_y):
                at = (m_sec * n_y + m_y) * piece
                for m_core, ref in ((0, keep_ref), (1, send_ref)):
                    part = acc[pl.ds(place(me, m_core, m_sec, m_y, n_sec, n_y, piece), piece), :]
                    ref[at : at + piece] = part.astype(ref.dtype)
    for store in stores:
        store.wait()


SCALARS = pl.BlockSpec(memory_space=pltpu.SMEM)
ARRAY = pl.BlockSpec(memory_space=pltpu.VMEM)
FAR = pl.BlockSpec(memory_space=pl.ANY)


def at_once(
    kernel, name, out_shape, out_specs, scratch, scalars, near, far, aliases=None, vmem=VMEM_LIMIT, nbytes=1000
):
    return pl.pallas_call(
        kernel,
        in_specs=[SCALARS] * len(scalars) + [ARRAY] * len(near) + [FAR] * len(far),
        out_specs=out_specs,
        out_shape=out_shape,
        scratch_shapes=scratch,
        input_output_aliases=aliases or {},
        name=name,
        compiler_params=pltpu.CompilerParams(vmem_limit_bytes=vmem),
        cost_estimate=pl.CostEstimate(flops=1000, bytes_accessed=nbytes, transcendentals=0),
    )(*scalars, *near, *far)


def absorb(me, counts, c_parts, begun, e_far, projectors):
    slices, rows, width = projectors.shape
    n, n_sec, n_y, piece = sizes(rows, width)
    per = 3 if slices % 3 == 0 else 1
    half = (width if piece % 16 else width // 2, width)
    held = (slices, rows, width)
    enlarged, keep, send = at_once(
        functools.partial(absorb_kernel, n, n_sec, piece, per),
        "absorb",
        [
            jax.ShapeDtypeStruct(held, BF16),
            jax.ShapeDtypeStruct(half, F32),
            jax.ShapeDtypeStruct(half, BF16),
        ],
        [FAR, ARRAY, ARRAY],
        [
            pltpu.VMEM((n - 3, *held), BF16),
            pltpu.VMEM(held, BF16),
            pltpu.VMEM((width, width), F32),
            pltpu.SemaphoreType.DMA((n - 3, slices // per)),
            pltpu.SemaphoreType.DMA((slices // per,)),
        ],
        (me, counts),
        (c_parts, projectors, begun, e_far[-1]),
        tuple(e_far[:-1]),
        vmem=16 * 1024 * 1024,
    )
    if piece % 16:
        keep = relative(keep, me, n_sec, n_y)[0]
        send = relative(send, me, n_sec, n_y)[1]
    shape = (n_sec, n_y * piece, width)
    return enlarged, keep.reshape(shape), send.reshape(shape)


def relative(value, me, n_sec, n_y):
    rows, cols = value.shape
    value = value.reshape(2, n_sec, n_y, rows // (2 * n_sec * n_y), cols)
    value = jnp.take(value, jnp.arange(2) ^ (me[0] & 1), axis=0)
    value = jnp.take(value, jnp.arange(n_sec) ^ me[1], axis=1)
    return jnp.take(value, jnp.arange(n_y) ^ (me[0] >> 1), axis=2).reshape(2, rows // 2, cols)


class Order:
    def __init__(self):
        self.last = None

    def __call__(self, step, *args):
        if self.last is not None:
            args = lax.optimization_barrier((*args, self.last))[:-1]
        out = step(*args)
        self.last = jax.tree.leaves(out)[0]
        return out


def add_core(keep, *arrived):
    arrived = [block for part in arrived for block in part]
    total = [keep[m] + arrived[m].astype(F32) for m in range(len(arrived))]
    return [block.astype(BF16) for block in total], total[0]


def add_sec(total, *arrived):
    for block in arrived:
        total = total + block.astype(F32)
    return total.astype(BF16)


def add_chips(own, *arrived):
    n_y = len(arrived) + 1
    total = own.astype(F32)
    for m, block in enumerate(arrived, 1):
        pieces = block.reshape(n_y, -1, block.shape[-1])
        block = jnp.concatenate([pieces[j ^ m] for j in range(n_y)], axis=0)
        total = total + block.astype(F32)
    return total.astype(BF16)


def to_sec(blocks):
    return [swap(blocks[m], "sec", m) for m in range(1, lax.axis_size("sec"))]


def to_chips(blocks):
    return [swap(blocks[m], "env", 2 * m) for m in range(1, lax.axis_size("env") // 2)]


def all_sec(block):
    return [block] + to_sec([block] * lax.axis_size("sec"))


def gradient_kernel(n, n_sec, piece, per, ahead, me, counts, *refs):
    blocks, refs = refs[: 2 * n_sec], refs[2 * n_sec :]
    p_ref, last_e, refs = refs[0], refs[1], refs[2:]
    cot_refs, far_refs, refs = refs[:n], refs[n : 2 * n - 1], refs[2 * n - 1 :]
    g_ref, own_ref, out, full, cot, held, grad, acc, sems, cot_sems = refs
    slices, rows, width = p_ref.shape
    cols = width // n_sec
    n_y = n // 2
    cot_copies = [
        pltpu.make_async_copy(cot_refs[m].at[pl.ds(ahead, rows)], cot.at[m], cot_sems.at[m])
        for m in range(n)
    ]
    for copy in cot_copies:
        copy.start()
    e_copies = [
        pltpu.make_async_copy(far_refs[m], held.at[m], sems.at[m]) for m in range(n - 1)
    ]
    for copy in e_copies:
        copy.start()
    e_refs = [*[held.at[m] for m in range(n - 1)], last_e]

    for m_core in range(2):
        for m_sec in range(n_sec):
            block = blocks[m_core * n_sec + m_sec]
            if piece % 16:
                at = (m_core * n_sec + m_sec) * n_y * piece
                full[at : at + n_y * piece] = block[...]
                continue
            for m_y in range(n_y):
                to = place(me, m_core, m_sec, m_y, n_sec, n_y, piece)
                full[pl.ds(to, piece), :] = block[m_y * piece : (m_y + 1) * piece]
    for copy in cot_copies:
        copy.wait()
    step = 16
    sums = (jnp.zeros((step, width), F32),) * 2

    def place_of(m, i):
        return pl.ds(pl.multiple_of((me[0] ^ m) * rows + i * step, step), step)

    def cot_of(m, i):
        return cot[m, pl.ds(pl.multiple_of(i * step, step), step), :].astype(F32)

    for m in range(n):

        def add(i, sums, m=m):
            x, c = full[place_of(m, i), :].astype(F32), cot_of(m, i)
            return sums[0] + x * x, sums[1] + c * x

        sums = lax.fori_loop(0, rows // step, add, sums, unroll=3)
    norm_sq = jnp.sum(sums[0], keepdims=True)
    cross = jnp.sum(sums[1], keepdims=True)
    scale = width / jnp.sqrt(norm_sq)
    ratio = scale * cross * scale / (width * width)
    for m in range(n):

        def write(i, _, m=m):
            x = full[place_of(m, i), :].astype(F32)
            g_ref[place_of(m, i), :] = (scale * (cot_of(m, i) - x * ratio)).astype(BF16)
            return _

        lax.fori_loop(0, rows // step, write, 0, unroll=3)
    own = full[pl.ds(pl.multiple_of(me[0] * rows, rows), rows), :]
    picked = own[:, :cols]
    for q in range(1, n_sec):
        picked = jnp.where(me[1] == q, own[:, q * cols : (q + 1) * cols], picked)
    own_ref[...] = picked.astype(F32) * scale

    for k in range(slices // per):
        x = dot(p_ref[k * per : k * per + per].reshape(per * rows, width), g_ref[...])
        for i in range(per):
            part = x[i * rows : (i + 1) * rows]
            keep = keep_columns(part.shape, 0, counts[k * per + i])
            grad[k * per + i] = jnp.where(keep, part, 0.0).astype(BF16)
    for copy in e_copies:
        copy.wait()
    for m in range(n):
        x = None
        for k in range(slices):
            y = dot(e_refs[m][k], grad[k], ((1,), (1,)))
            x = y if x is None else x + y
        acc[pl.ds(pl.multiple_of((me[0] ^ m) * rows, rows), rows), :] = x
    for m in range(n_sec):
        at = pl.multiple_of((me[1] ^ m) * cols, cols)
        out[m] = acc[pl.ds(at, cols), :].astype(BF16).T


def gradient(me, counts, halves, cots, ahead, projectors, e_blocks):
    slices, rows, width = projectors.shape
    n, n_sec, _, piece = sizes(rows, width)
    per = 3 if slices % 3 == 0 else 1
    cols = width // n_sec
    held = (slices, rows, width)
    return at_once(
        functools.partial(gradient_kernel, n, n_sec, piece, per, ahead),
        "gradient",
        [
            jax.ShapeDtypeStruct((width, width), BF16),
            jax.ShapeDtypeStruct((rows, cols), F32),
            jax.ShapeDtypeStruct((n_sec, rows, cols), BF16),
        ],
        [ARRAY] * 3,
        [
            pltpu.VMEM((width, width), BF16),
            pltpu.VMEM((n, rows, width), BF16),
            pltpu.VMEM((n - 1, *held), BF16),
            pltpu.VMEM(held, BF16),
            pltpu.VMEM((width, rows), F32),
            pltpu.SemaphoreType.DMA((n - 1,)),
            pltpu.SemaphoreType.DMA((n,)),
        ],
        (me, counts),
        (*halves, projectors, e_blocks[-1]),
        (*cots, *e_blocks[:-1]),
        vmem=24 * 1024 * 1024,
        nbytes=20 * slices * rows * width,
    )


def outputs_kernel(per, dims, counts, g_ref, x_ref, out, held, sems):
    slices, rows, width = x_ref.shape
    stores = []
    for k in range(slices // per):
        at = pl.ds(k * per, per)
        y = dot(x_ref[k * per : k * per + per].reshape(per * rows, width), g_ref[...], dims)
        for i in range(per):
            part = y[i * rows : (i + 1) * rows]
            if dims[1] == (0,):
                keep = keep_columns(part.shape, 0, counts[k * per + i])
                part = jnp.where(keep, part, 0.0)
            held[k * per + i] = part
        stores.append(pltpu.make_async_copy(held.at[at], out.at[at], sems.at[k]))
        stores[-1].start()
    for copy in stores:
        copy.wait()


def outputs(name, counts, g, x, slices, dims):
    count, rows, width = x.shape
    per = 3 if count % 3 == 0 else 2 if count % 2 == 0 else 1
    return at_once(
        functools.partial(outputs_kernel, per, dims),
        name,
        jax.ShapeDtypeStruct((slices, rows, width), F32),
        FAR,
        [pltpu.VMEM((count, rows, width), F32), pltpu.SemaphoreType.DMA((count // per,))],
        (counts,),
        (g, x),
        (),
        vmem=24 * 1024 * 1024,
    )


def mix_kernel(n, slices, rows, c_ref, begun, *refs):
    across = [c_ref[m].T for m in range(n - 2)]
    for i in range(slices):
        y = begun[i]
        for m in range(n - 2):
            y = y + dot(across[m], refs[m][i * rows : (i + 1) * rows])
        refs[-1][i] = y.astype(BF16)


def mix(c_far, begun, p_far):
    slices, rows, width = begun.shape
    return call(
        functools.partial(mix_kernel, c_far.shape[0] + 2, slices, rows),
        "mix",
        (1,),
        [whole(c_far.shape), group(slices, (rows, width))]
        + [whole((slices * rows, width))] * len(p_far),
        group(slices, (rows, width)),
        jax.ShapeDtypeStruct((slices, rows, width), BF16),
        [],
        0,
        0,
        0,
        (c_far, begun, *p_far),
    )


def spans(slices, per):
    return [(at, min(per, slices - at)) for at in range(0, slices, per)]


def add_far_kernel(n, per, c_ref, begun, *refs):
    across = [c_ref[m].T for m in range(n - 3)]
    for i in range(per):
        y = begun[i]
        for m in range(n - 3):
            y = y + dot(across[m], refs[m][i])
        refs[-1][i] = y


def add_far(c_far, begun, far):
    slices, rows, width = begun.shape
    n = c_far.shape[0] + 2
    per = 3 if slices % 3 == 0 else 1
    return call(
        functools.partial(add_far_kernel, n, per),
        "add_far",
        (slices // per,),
        [whole(c_far.shape)] + [group(per, (rows, width))] * (n - 2),
        group(per, (rows, width)),
        jax.ShapeDtypeStruct((slices, rows, width), F32),
        [],
        0,
        0,
        0,
        (c_far, begun, *far),
    )


def late_kernel(first, groups, counts, g_ref, c_ref, begun, fwd, _, out, q, x, out_sems):
    slices, rows, width = begun.shape
    across = c_ref[...].T
    stores = []
    for k, (at, size) in enumerate(groups):
        for i in range(size):
            y = begun[at + i] + dot(across, fwd[at + i])
            q[i * rows : (i + 1) * rows] = y.astype(BF16)
        y = dot(q[: size * rows], g_ref[...])
        for i in range(size):
            part = y[i * rows : (i + 1) * rows]
            keep = keep_columns(part.shape, 0, counts[first + at + i])
            x[at + i] = jnp.where(keep, part, 0.0)
        to = out.at[pl.ds(first + at, size)]
        stores.append(pltpu.make_async_copy(x.at[pl.ds(at, size)], to, out_sems.at[k]))
        stores[-1].start()
    for store in stores:
        store.wait()


def late_edge_gradient(result, counts, g, c_last, begun, fwd, first):
    slices, rows, width = begun.shape
    groups = spans(slices, 2)
    return at_once(
        functools.partial(late_kernel, first, groups),
        "late_edge_gradient",
        jax.ShapeDtypeStruct(result.shape, F32),
        FAR,
        [
            pltpu.VMEM((2 * rows, width), BF16),
            pltpu.VMEM((slices, rows, width), F32),
            pltpu.SemaphoreType.DMA((len(groups),)),
        ],
        (counts,),
        (g, c_last, begun, fwd),
        (result,),
        {5: 0},
        vmem=16 * 1024 * 1024,
    )


def cotangent_order(*blocks):
    n_sec, s = lax.axis_size("sec"), lax.axis_index("sec")
    ordered = []
    for q in range(n_sec):
        block = blocks[0]
        for m in range(1, n_sec):
            block = jnp.where((s ^ m) == q, blocks[m], block)
        ordered.append(block)
    return jnp.concatenate(ordered, axis=1)


def per_device(corner, edges, projectors, tile_counts, cotangent):
    n, n_sec = lax.axis_size("env"), lax.axis_size("sec")
    e, s = lax.axis_index("env"), lax.axis_index("sec")
    slices, rows, width = edges.shape
    cols = cotangent.shape[1]
    piece = width // (n * n_sec)
    me = jnp.stack([e, s]).astype(jnp.int32)
    core, y = e & 1, e >> 1

    def from_chips(value):
        return to_chips([value] * (n // 2))

    def both_cores(arrived):
        return [b for block in arrived for b in (block, swap(block, "env", 1))]

    def barrier(value, *earlier):
        return lax.optimization_barrier((value, earlier))[0]

    far = from_chips(edges)
    cot = cotangent.astype(BF16)
    cot = cotangent_order(cot, *to_sec([cot] * n_sec))
    early = max(slices // 3, 1)
    ahead = early * rows

    def first_piece(m):
        block = lax.dynamic_slice_in_dim(corner, (y ^ m) * 2 * rows, 2 * rows, 1)
        block = jnp.concatenate([block[: rows // 2], block[rows // 2 :]], axis=1)
        block = jnp.pad(block, ((0, 0), (0, width - block.shape[1])))
        return jnp.concatenate([projectors[:early].reshape(ahead, width), cot, block], axis=0)

    first = [first_piece(m) for m in range(n // 2)]
    second = projectors[early:]
    near = [swap(first[0], "env", 1), swap(second, "env", 1)]
    c_parts = jnp.stack(
        [lax.dynamic_slice_in_dim(corner, (e ^ m) * rows, rows, 1) for m in range(n)]
    )
    e_near = swap(edges, "env", 1)
    begun = begin(c_parts, edges, e_near)

    def corner_columns(piece):
        block = piece[ahead + rows :]
        block = jnp.concatenate([block[:, : 2 * rows], block[:, 2 * rows : 4 * rows]], axis=0)
        return lax.dynamic_slice_in_dim(block, core * rows, rows, 1)

    c_near = jnp.stack([corner_columns(first[0]).T, corner_columns(near[0]).T])
    near_early = near[0][:ahead].reshape(early, rows, width)
    mixing = [
        begin(c_near, projectors[:early], near_early),
        begin(c_near, second, near[1]),
    ]
    far = barrier(far, begun, mixing)
    p_far = to_chips(first)
    e_blocks = [edges, e_near, *both_cores(far)]

    order = Order()

    enlarged, keep, send = order(
        lambda *f: absorb(me, tile_counts, c_parts, begun, f, projectors), *e_blocks[2:])
    half = n_sec // 2
    moved, total = order(
        add_core, keep, swap(send[:half], "env", 1), swap(send[half:], "env", 1))
    sec = to_sec(moved)
    total = barrier(total, p_far)
    some = order(add_sec, total, *sec)
    some = order(add_chips, some, *from_chips(some))
    half = all_sec(some)
    second_far = from_chips(barrier(second, some))
    p_far = both_cores(barrier(p_far, some))
    cots = [first[0], near[0], *p_far]
    c_far = jnp.stack([corner_columns(p) for p in p_far])
    q = order(lambda c: mix(c, mixing[0], p_far), c_far)
    half = barrier(half, order.last)
    halves = half + [swap(h, "env", 1) for h in half]
    if piece % 16:
        halves = list(
            relative(jnp.concatenate(halves), me, n_sec, n // 2).reshape(2 * n_sec, -1, width))
    g, corner_new, part = order(
        lambda *h: gradient(me, tile_counts, h, cots, ahead, projectors, e_blocks), *halves)
    moved = to_sec(part)
    proj_grad = order(
        lambda g: outputs(
            "proj_gradient", tile_counts, g, enlarged, slices, ((1,), (1,))), g)
    edge_grad = order(
        lambda g: outputs("edge_gradient", tile_counts, g, q, slices, ((1,), (0,))), g)
    corner_grad = order(
        lambda *b: sum((x.astype(F32) for x in b[1:]), b[0].astype(F32)), part[0], *moved)
    p_far = both_cores(barrier(second_far, corner_grad))
    begun = order(lambda b, *p: add_far(c_far, b, p), mixing[1], *p_far[:-1])
    edge_grad = order(
        lambda r, b, p: late_edge_gradient(r, tile_counts, g, c_far[-1], b, p, early),
        edge_grad, begun, p_far[-1])
    return (corner_new, corner_grad, edge_grad, proj_grad)


def solution(mesh):
    placed = (
        P(("sweep", "env"), None),
        P(("sweep", "sec"), "env", None),
        P(("sweep", "sec"), "env", None),
        P(("sweep", "sec")),
        P(("sweep", "env"), "sec"),
    )
    return jax.shard_map(
        per_device,
        mesh=mesh,
        in_specs=placed,
        out_specs=(
            P(("sweep", "env"), "sec"),
            P(("sweep", "env"), "sec"),
            P(("sweep", "sec"), "env", None),
            P(("sweep", "sec"), "env", None),
        ),
        check_vma=False,
    )
```

```python
import functools

import jax
import jax.numpy as jnp
from jax import lax
from jax.experimental import pallas as pl
from jax.experimental.pallas import tpu as pltpu
from jax.sharding import PartitionSpec as P

TILE = 128
F32, BF16 = jnp.float32, jnp.bfloat16
VMEM_LIMIT = 40 * 1024 * 1024


def swap(value, axis, offset):
    size = lax.axis_size(axis)
    return lax.ppermute(value, axis, [(i, i ^ offset) for i in range(size)])


def after(value, *earlier):
    return lax.optimization_barrier((value, *earlier))[0]


def dot(a, b, dims=((1,), (0,))):
    return lax.dot_general(a, b, (dims, ((), ())), preferred_element_type=F32)


def call(kernel, name, grid, in_specs, out_specs, out_shape, scratch, flops, nbytes, prefetch, args):
    return pl.pallas_call(
        kernel,
        grid_spec=pltpu.PrefetchScalarGridSpec(
            num_scalar_prefetch=prefetch,
            grid=grid,
            in_specs=in_specs,
            out_specs=out_specs,
            scratch_shapes=scratch,
        ),
        out_shape=out_shape,
        name=name,
        compiler_params=pltpu.CompilerParams(vmem_limit_bytes=VMEM_LIMIT),
        cost_estimate=pl.CostEstimate(flops=1000, bytes_accessed=1000, transcendentals=0),
    )(*args)


def keep_columns(shape, first, count):
    return lax.broadcasted_iota(jnp.int32, shape, 1) + first < count * TILE


def whole(shape):
    return pl.BlockSpec(shape, lambda k, *s: (0,) * len(shape))


def group(size, shape, column=0, first=0):
    return pl.BlockSpec((size, *shape), lambda k, *s: (k + first, 0, column))


def sizes(mesh_rows, width):
    n, n_sec = lax.axis_size("env"), lax.axis_size("sec")
    return n, n_sec, n // 2, width // (n * n_sec)


def place(me, m_core, m_sec, m_y, n_sec, n_y, piece):
    core, y = me[0] & 1, me[0] >> 1
    at = (((core ^ m_core) * n_sec + (me[1] ^ m_sec)) * n_y + (y ^ m_y)) * piece
    return pl.multiple_of(at, piece)


def fetch(per, ref, buffer, rows, sems):
    copies = []
    for k in range(ref.shape[0] // per):
        at = pl.ds(k * per, per)
        copies.append(pltpu.make_async_copy(ref.at[at], buffer.at[at, rows], sems.at[k]))
        copies[-1].start()
    return copies


def begin_kernel(per, c_ref, own, near, out):
    for i in range(per):
        out[i] = dot(c_ref[0], own[i]) + dot(c_ref[1], near[i])


def begin(c_parts, own, near):
    slices, rows, width = own.shape
    per = 3 if slices % 3 == 0 else 1
    return call(
        functools.partial(begin_kernel, per),
        "begin",
        (slices // per,),
        [whole(c_parts.shape)] + [group(per, (rows, width))] * 2,
        group(per, (c_parts.shape[1], width)),
        jax.ShapeDtypeStruct((slices, c_parts.shape[1], width), F32),
        [],
        0,
        0,
        0,
        (c_parts, own, near),
    )


def absorb_kernel(n, n_sec, piece, per, me, counts, c_ref, p_ref, begun, fwd, *refs):
    far_refs, (enl_ref, keep_ref, send_ref, held, enl, acc, sems, out_sems) = refs[:-8], refs[-8:]
    n_y = n // 2
    slices, rows, width = p_ref.shape
    copies = [
        fetch(per, far_refs[m], held.at[m], pl.ds(0, rows), sems.at[m]) for m in range(n - 3)
    ]
    stores = []
    for k in range(slices // per):
        at = pl.ds(k * per, per)
        for m in range(n - 3):
            copies[m][k].wait()
        for i in range(k * per, k * per + per):
            x = begun[i] + dot(c_ref[n - 1], fwd[i])
            for m in range(n - 3):
                x = x + dot(c_ref[2 + m], held[m, i])
            enl[i] = jnp.where(keep_columns(x.shape, 0, counts[i]), x, 0.0).astype(BF16)
        stores.append(pltpu.make_async_copy(enl.at[at], enl_ref.at[at], out_sems.at[k]))
        stores[-1].start()
    half = width // 2
    for first in (0, half):
        acc[first : first + half, :] = dot(
            p_ref[:, :, first : first + half].reshape(slices * rows, half),
            enl[...].reshape(slices * rows, width),
            ((0,), (0,)),
        )
    if piece % 16:
        keep_ref[...] = acc[...]
        send_ref[...] = acc[...].astype(BF16)
    else:
        for m_sec in range(n_sec):
            for m_y in range(n_y):
                at = (m_sec * n_y + m_y) * piece
                for m_core, ref in ((0, keep_ref), (1, send_ref)):
                    part = acc[pl.ds(place(me, m_core, m_sec, m_y, n_sec, n_y, piece), piece), :]
                    ref[at : at + piece] = part.astype(ref.dtype)
    for store in stores:
        store.wait()


SCALARS = pl.BlockSpec(memory_space=pltpu.SMEM)
ARRAY = pl.BlockSpec(memory_space=pltpu.VMEM)
FAR = pl.BlockSpec(memory_space=pl.ANY)


def at_once(
    kernel, name, out_shape, out_specs, scratch, scalars, near, far, aliases=None, vmem=VMEM_LIMIT, nbytes=1000
):
    return pl.pallas_call(
        kernel,
        in_specs=[SCALARS] * len(scalars) + [ARRAY] * len(near) + [FAR] * len(far),
        out_specs=out_specs,
        out_shape=out_shape,
        scratch_shapes=scratch,
        input_output_aliases=aliases or {},
        name=name,
        compiler_params=pltpu.CompilerParams(vmem_limit_bytes=vmem),
        cost_estimate=pl.CostEstimate(flops=1000, bytes_accessed=nbytes, transcendentals=0),
    )(*scalars, *near, *far)


def absorb(me, counts, c_parts, begun, e_far, projectors):
    slices, rows, width = projectors.shape
    n, n_sec, n_y, piece = sizes(rows, width)
    per = 3 if slices % 3 == 0 else 1
    half = (width if piece % 16 else width // 2, width)
    held = (slices, rows, width)
    enlarged, keep, send = at_once(
        functools.partial(absorb_kernel, n, n_sec, piece, per),
        "absorb",
        [
            jax.ShapeDtypeStruct(held, BF16),
            jax.ShapeDtypeStruct(half, F32),
            jax.ShapeDtypeStruct(half, BF16),
        ],
        [FAR, ARRAY, ARRAY],
        [
            pltpu.VMEM((n - 3, *held), BF16),
            pltpu.VMEM(held, BF16),
            pltpu.VMEM((width, width), F32),
            pltpu.SemaphoreType.DMA((n - 3, slices // per)),
            pltpu.SemaphoreType.DMA((slices // per,)),
        ],
        (me, counts),
        (c_parts, projectors, begun, e_far[-1]),
        tuple(e_far[:-1]),
        vmem=16 * 1024 * 1024,
    )
    if piece % 16:
        keep = relative(keep, me, n_sec, n_y)[0]
        send = relative(send, me, n_sec, n_y)[1]
    shape = (n_sec, n_y * piece, width)
    return enlarged, keep.reshape(shape), send.reshape(shape)


def relative(value, me, n_sec, n_y):
    rows, cols = value.shape
    value = value.reshape(2, n_sec, n_y, rows // (2 * n_sec * n_y), cols)
    value = jnp.take(value, jnp.arange(2) ^ (me[0] & 1), axis=0)
    value = jnp.take(value, jnp.arange(n_sec) ^ me[1], axis=1)
    return jnp.take(value, jnp.arange(n_y) ^ (me[0] >> 1), axis=2).reshape(2, rows // 2, cols)


class Order:
    def __init__(self):
        self.last = None

    def __call__(self, step, *args):
        if self.last is not None:
            args = lax.optimization_barrier((*args, self.last))[:-1]
        out = step(*args)
        self.last = jax.tree.leaves(out)[0]
        return out


def add_core(keep, *arrived):
    arrived = [block for part in arrived for block in part]
    total = [keep[m] + arrived[m].astype(F32) for m in range(len(arrived))]
    return [block.astype(BF16) for block in total], total[0]


def add_sec(total, *arrived):
    for block in arrived:
        total = total + block.astype(F32)
    return total.astype(BF16)


def add_chips(own, *arrived):
    n_y = len(arrived) + 1
    total = own.astype(F32)
    for m, block in enumerate(arrived, 1):
        pieces = block.reshape(n_y, -1, block.shape[-1])
        block = jnp.concatenate([pieces[j ^ m] for j in range(n_y)], axis=0)
        total = total + block.astype(F32)
    return total.astype(BF16)


def to_sec(blocks):
    return [swap(blocks[m], "sec", m) for m in range(1, lax.axis_size("sec"))]


def to_chips(blocks):
    return [swap(blocks[m], "env", 2 * m) for m in range(1, lax.axis_size("env") // 2)]


def all_sec(block):
    return [block] + to_sec([block] * lax.axis_size("sec"))


def gradient_kernel(n, n_sec, piece, per, ahead, me, counts, *refs):
    blocks, refs = refs[: 2 * n_sec], refs[2 * n_sec :]
    p_ref, last_e, refs = refs[0], refs[1], refs[2:]
    cot_refs, far_refs, refs = refs[:n], refs[n : 2 * n - 1], refs[2 * n - 1 :]
    g_ref, own_ref, out, full, cot, held, grad, acc, sems, cot_sems = refs
    slices, rows, width = p_ref.shape
    cols = width // n_sec
    n_y = n // 2
    cot_copies = [
        pltpu.make_async_copy(cot_refs[m].at[pl.ds(ahead, rows)], cot.at[m], cot_sems.at[m])
        for m in range(n)
    ]
    for copy in cot_copies:
        copy.start()
    e_copies = [
        pltpu.make_async_copy(far_refs[m], held.at[m], sems.at[m]) for m in range(n - 1)
    ]
    for copy in e_copies:
        copy.start()
    e_refs = [*[held.at[m] for m in range(n - 1)], last_e]

    for m_core in range(2):
        for m_sec in range(n_sec):
            block = blocks[m_core * n_sec + m_sec]
            if piece % 16:
                at = (m_core * n_sec + m_sec) * n_y * piece
                full[at : at + n_y * piece] = block[...]
                continue
            for m_y in range(n_y):
                to = place(me, m_core, m_sec, m_y, n_sec, n_y, piece)
                full[pl.ds(to, piece), :] = block[m_y * piece : (m_y + 1) * piece]
    for copy in cot_copies:
        copy.wait()
    step = 16
    sums = (jnp.zeros((step, width), F32),) * 2

    def place_of(m, i):
        return pl.ds(pl.multiple_of((me[0] ^ m) * rows + i * step, step), step)

    def cot_of(m, i):
        return cot[m, pl.ds(pl.multiple_of(i * step, step), step), :].astype(F32)

    for m in range(n):

        def add(i, sums, m=m):
            x, c = full[place_of(m, i), :].astype(F32), cot_of(m, i)
            return sums[0] + x * x, sums[1] + c * x

        sums = lax.fori_loop(0, rows // step, add, sums, unroll=3)
    norm_sq = jnp.sum(sums[0], keepdims=True)
    cross = jnp.sum(sums[1], keepdims=True)
    scale = width / jnp.sqrt(norm_sq)
    ratio = scale * cross * scale / (width * width)
    for m in range(n):

        def write(i, _, m=m):
            x = full[place_of(m, i), :].astype(F32)
            g_ref[place_of(m, i), :] = (scale * (cot_of(m, i) - x * ratio)).astype(BF16)
            return _

        lax.fori_loop(0, rows // step, write, 0, unroll=3)
    own = full[pl.ds(pl.multiple_of(me[0] * rows, rows), rows), :]
    picked = own[:, :cols]
    for q in range(1, n_sec):
        picked = jnp.where(me[1] == q, own[:, q * cols : (q + 1) * cols], picked)
    own_ref[...] = picked.astype(F32) * scale

    x = dot(p_ref[...].reshape(slices * rows, width), g_ref[...])
    for k in range(slices):
        part = x[k * rows : (k + 1) * rows]
        grad[k] = jnp.where(keep_columns(part.shape, 0, counts[k]), part, 0.0).astype(BF16)
    for copy in e_copies:
        copy.wait()
    for m in range(n):
        x = None
        for k in range(slices):
            y = dot(e_refs[m][k], grad[k], ((1,), (1,)))
            x = y if x is None else x + y
        acc[pl.ds(pl.multiple_of((me[0] ^ m) * rows, rows), rows), :] = x
    for m in range(n_sec):
        at = pl.multiple_of((me[1] ^ m) * cols, cols)
        out[m] = acc[pl.ds(at, cols), :].astype(BF16).T


def gradient(me, counts, halves, cots, ahead, projectors, e_blocks):
    slices, rows, width = projectors.shape
    n, n_sec, _, piece = sizes(rows, width)
    per = 3 if slices % 3 == 0 else 1
    cols = width // n_sec
    held = (slices, rows, width)
    return at_once(
        functools.partial(gradient_kernel, n, n_sec, piece, per, ahead),
        "gradient",
        [
            jax.ShapeDtypeStruct((width, width), BF16),
            jax.ShapeDtypeStruct((rows, cols), F32),
            jax.ShapeDtypeStruct((n_sec, rows, cols), BF16),
        ],
        [ARRAY] * 3,
        [
            pltpu.VMEM((width, width), BF16),
            pltpu.VMEM((n, rows, width), BF16),
            pltpu.VMEM((n - 1, *held), BF16),
            pltpu.VMEM(held, BF16),
            pltpu.VMEM((width, rows), F32),
            pltpu.SemaphoreType.DMA((n - 1,)),
            pltpu.SemaphoreType.DMA((n,)),
        ],
        (me, counts),
        (*halves, projectors, e_blocks[-1]),
        (*cots, *e_blocks[:-1]),
        vmem=24 * 1024 * 1024,
        nbytes=20 * slices * rows * width,
    )


def outputs_kernel(per, dims, counts, g_ref, x_ref, out, held, sems):
    slices, rows, width = x_ref.shape
    stores = []
    for k in range(slices // per):
        at = pl.ds(k * per, per)
        y = dot(x_ref[k * per : k * per + per].reshape(per * rows, width), g_ref[...], dims)
        for i in range(per):
            part = y[i * rows : (i + 1) * rows]
            if dims[1] == (0,):
                keep = keep_columns(part.shape, 0, counts[k * per + i])
                part = jnp.where(keep, part, 0.0)
            held[k * per + i] = part
        stores.append(pltpu.make_async_copy(held.at[at], out.at[at], sems.at[k]))
        stores[-1].start()
    for copy in stores:
        copy.wait()


def outputs(name, counts, g, x, slices, dims):
    count, rows, width = x.shape
    per = 3 if count % 3 == 0 else 2 if count % 2 == 0 else 1
    return at_once(
        functools.partial(outputs_kernel, per, dims),
        name,
        jax.ShapeDtypeStruct((slices, rows, width), F32),
        FAR,
        [pltpu.VMEM((count, rows, width), F32), pltpu.SemaphoreType.DMA((count // per,))],
        (counts,),
        (g, x),
        (),
        vmem=24 * 1024 * 1024,
    )


def mix_kernel(n, slices, rows, c_ref, begun, *refs):
    across = [c_ref[m].T for m in range(n - 2)]
    for i in range(slices):
        y = begun[i]
        for m in range(n - 2):
            y = y + dot(across[m], refs[m][i * rows : (i + 1) * rows])
        refs[-1][i] = y.astype(BF16)


def mix(c_far, begun, p_far):
    slices, rows, width = begun.shape
    return call(
        functools.partial(mix_kernel, c_far.shape[0] + 2, slices, rows),
        "mix",
        (1,),
        [whole(c_far.shape), group(slices, (rows, width))]
        + [whole((slices * rows, width))] * len(p_far),
        group(slices, (rows, width)),
        jax.ShapeDtypeStruct((slices, rows, width), BF16),
        [],
        0,
        0,
        0,
        (c_far, begun, *p_far),
    )


def spans(slices, per):
    return [(at, min(per, slices - at)) for at in range(0, slices, per)]


def add_far_kernel(n, per, c_ref, begun, *refs):
    across = [c_ref[m].T for m in range(n - 3)]
    for i in range(per):
        y = begun[i]
        for m in range(n - 3):
            y = y + dot(across[m], refs[m][i])
        refs[-1][i] = y


def add_far(c_far, begun, far):
    slices, rows, width = begun.shape
    n = c_far.shape[0] + 2
    per = 3 if slices % 3 == 0 else 1
    return call(
        functools.partial(add_far_kernel, n, per),
        "add_far",
        (slices // per,),
        [whole(c_far.shape)] + [group(per, (rows, width))] * (n - 2),
        group(per, (rows, width)),
        jax.ShapeDtypeStruct((slices, rows, width), F32),
        [],
        0,
        0,
        0,
        (c_far, begun, *far),
    )


def late_kernel(first, groups, counts, g_ref, c_ref, begun, fwd, _, out, q, x, out_sems):
    slices, rows, width = begun.shape
    across = c_ref[...].T
    stores = []
    for k, (at, size) in enumerate(groups):
        for i in range(size):
            y = begun[at + i] + dot(across, fwd[at + i])
            q[i * rows : (i + 1) * rows] = y.astype(BF16)
        y = dot(q[: size * rows], g_ref[...])
        for i in range(size):
            part = y[i * rows : (i + 1) * rows]
            keep = keep_columns(part.shape, 0, counts[first + at + i])
            x[at + i] = jnp.where(keep, part, 0.0)
        to = out.at[pl.ds(first + at, size)]
        stores.append(pltpu.make_async_copy(x.at[pl.ds(at, size)], to, out_sems.at[k]))
        stores[-1].start()
    for store in stores:
        store.wait()


def late_edge_gradient(result, counts, g, c_last, begun, fwd, first):
    slices, rows, width = begun.shape
    groups = spans(slices, 2)
    return at_once(
        functools.partial(late_kernel, first, groups),
        "late_edge_gradient",
        jax.ShapeDtypeStruct(result.shape, F32),
        FAR,
        [
            pltpu.VMEM((2 * rows, width), BF16),
            pltpu.VMEM((slices, rows, width), F32),
            pltpu.SemaphoreType.DMA((len(groups),)),
        ],
        (counts,),
        (g, c_last, begun, fwd),
        (result,),
        {5: 0},
        vmem=16 * 1024 * 1024,
    )


def cotangent_order(*blocks):
    n_sec, s = lax.axis_size("sec"), lax.axis_index("sec")
    ordered = []
    for q in range(n_sec):
        block = blocks[0]
        for m in range(1, n_sec):
            block = jnp.where((s ^ m) == q, blocks[m], block)
        ordered.append(block)
    return jnp.concatenate(ordered, axis=1)


def per_device(corner, edges, projectors, tile_counts, cotangent):
    n, n_sec = lax.axis_size("env"), lax.axis_size("sec")
    e, s = lax.axis_index("env"), lax.axis_index("sec")
    slices, rows, width = edges.shape
    cols = cotangent.shape[1]
    piece = width // (n * n_sec)
    me = jnp.stack([e, s]).astype(jnp.int32)
    core, y = e & 1, e >> 1

    def from_chips(value):
        return to_chips([value] * (n // 2))

    def both_cores(arrived):
        return [b for block in arrived for b in (block, swap(block, "env", 1))]

    def barrier(value, *earlier):
        return lax.optimization_barrier((value, earlier))[0]

    far = from_chips(edges)
    cot = cotangent.astype(BF16)
    cot = cotangent_order(cot, *to_sec([cot] * n_sec))
    early = max(slices // 3, 1)
    ahead = early * rows

    def first_piece(m):
        block = lax.dynamic_slice_in_dim(corner, (y ^ m) * 2 * rows, 2 * rows, 1)
        block = jnp.concatenate([block[: rows // 2], block[rows // 2 :]], axis=1)
        block = jnp.pad(block, ((0, 0), (0, width - block.shape[1])))
        return jnp.concatenate([projectors[:early].reshape(ahead, width), cot, block], axis=0)

    first = [first_piece(m) for m in range(n // 2)]
    second = projectors[early:]
    near = [swap(first[0], "env", 1), swap(second, "env", 1)]
    c_parts = jnp.stack(
        [lax.dynamic_slice_in_dim(corner, (e ^ m) * rows, rows, 1) for m in range(n)]
    )
    e_near = swap(edges, "env", 1)
    begun = begin(c_parts, edges, e_near)

    def corner_columns(piece):
        block = piece[ahead + rows :]
        block = jnp.concatenate([block[:, : 2 * rows], block[:, 2 * rows : 4 * rows]], axis=0)
        return lax.dynamic_slice_in_dim(block, core * rows, rows, 1)

    c_near = jnp.stack([corner_columns(first[0]).T, corner_columns(near[0]).T])
    near_early = near[0][:ahead].reshape(early, rows, width)
    mixing = [
        begin(c_near, projectors[:early], near_early),
        begin(c_near, second, near[1]),
    ]
    far = barrier(far, begun, mixing)
    p_far = to_chips(first)
    e_blocks = [edges, e_near, *both_cores(far)]

    order = Order()

    enlarged, keep, send = order(
        lambda *f: absorb(me, tile_counts, c_parts, begun, f, projectors), *e_blocks[2:])
    half = n_sec // 2
    moved, total = order(
        add_core, keep, swap(send[:half], "env", 1), swap(send[half:], "env", 1))
    sec = to_sec(moved)
    total = barrier(total, p_far)
    some = order(add_sec, total, *sec)
    some = order(add_chips, some, *from_chips(some))
    half = all_sec(some)
    second_far = from_chips(barrier(second, some))
    p_far = both_cores(barrier(p_far, some))
    cots = [first[0], near[0], *p_far]
    c_far = jnp.stack([corner_columns(p) for p in p_far])
    q = order(lambda c: mix(c, mixing[0], p_far), c_far)
    half = barrier(half, order.last)
    halves = half + [swap(h, "env", 1) for h in half]
    if piece % 16:
        halves = list(
            relative(jnp.concatenate(halves), me, n_sec, n // 2).reshape(2 * n_sec, -1, width))
    g, corner_new, part = order(
        lambda *h: gradient(me, tile_counts, h, cots, ahead, projectors, e_blocks), *halves)
    moved = to_sec(part)
    proj_grad = order(
        lambda g: outputs(
            "proj_gradient", tile_counts, g, enlarged, slices, ((1,), (1,))), g)
    edge_grad = order(
        lambda g: outputs("edge_gradient", tile_counts, g, q, slices, ((1,), (0,))), g)
    corner_grad = order(
        lambda *b: sum((x.astype(F32) for x in b[1:]), b[0].astype(F32)), part[0], *moved)
    p_far = both_cores(barrier(second_far, corner_grad))
    begun = order(lambda b, *p: add_far(c_far, b, p), mixing[1], *p_far[:-1])
    edge_grad = order(
        lambda r, b, p: late_edge_gradient(r, tile_counts, g, c_far[-1], b, p, early),
        edge_grad, begun, p_far[-1])
    return (corner_new, corner_grad, edge_grad, proj_grad)


def solution(mesh):
    placed = (
        P(("sweep", "env"), None),
        P(("sweep", "sec"), "env", None),
        P(("sweep", "sec"), "env", None),
        P(("sweep", "sec")),
        P(("sweep", "env"), "sec"),
    )
    return jax.shard_map(
        per_device,
        mesh=mesh,
        in_specs=placed,
        out_specs=(
            P(("sweep", "env"), "sec"),
            P(("sweep", "env"), "sec"),
            P(("sweep", "sec"), "env", None),
            P(("sweep", "sec"), "env", None),
        ),
        check_vma=False,
    )
```
